512 devices in a mesh: helix: 32 (over z_lo, y), cross: 4 (over x), cls: 4 (over z_hi, core).
Axes of the slice: x: 4, y: 4, z: 16 (z_hi: 2, z_lo: 8; z = z_hi * 8 + z_lo), core: 2. Of those that a mesh axis runs over, the one named last changes fastest.
Arguments:
- concentration: float32 [64, 1024, 4096], P('cls', 'helix', 'cross'), may hold values from 0 to 0.9, as said below
- class_table: int32 [64], P('cls'), may hold values from 0 to 63, as said below
- settle_speed: float32 [64], replicated, may hold values from 0.05 to 2
- along_speed: float32 [1024, 4096], P('helix', 'cross'), may hold values from 0.2 to 1
- across_speed: float32 [1024, 4096], P('helix', 'cross'), may hold values from -0.5 to 0.5
- film_depth: float32 [1024, 4096], P('helix', 'cross'), may hold values from 0.5 to 2
- cell_mask: int32 [1024, 4096], P('helix', 'cross'), may hold values from 0 to 2
Outputs:
- advanced: float32 [64, 1024, 4096], P('cls', 'helix', 'cross')
The draws below stay inside these ranges and needn't reach their ends.
Inputs may be any that keep to these rules, and one draw needn't show every extreme that they name: `concentration`: every entry is nonnegative, and the sum over all 64 slots of a cell stays below 58. `class_table`: each class 0 .. 63 is held in exactly one slot.
All inputs are finite; a program needn't handle non-finite values.
Results may differ from the reference program's by a relative error of at most 0.00002.
Values sent between devices are 32-bit elements; how exact they have to be, the bound alone decides.
A program may use at most 64 MiB of HBM per device.

```python
import math
import jax
import jax.numpy as jnp
from jax import lax

CLASSES = 64
ROWS = 1024
COLS = 4096


def shared_classes(key):
    table = jax.random.permutation(jax.random.fold_in(key, 101), CLASSES).astype(jnp.int32)
    raw = jax.random.uniform(jax.random.fold_in(key, 102), (CLASSES,), jnp.float32)
    level = (raw - jnp.min(raw)) / (jnp.max(raw) - jnp.min(raw))
    return (table, level)


def draw_class_table(key, part):
    table, level = shared_classes(key)
    return table


def draw_settle_speed(key, part):
    table, level = shared_classes(key)
    speeds = 0.05 * jnp.exp(jnp.log(40.0) * level)
    return jnp.clip(speeds, 0.05, 2.0)


def draw_concentration(key, part):
    table, level = shared_classes(key)
    key = jax.random.fold_in(key, 11)
    slot_level = level[table]
    tilt_key, load_key, amp_key = jax.random.split(key, 3)
    block_tilt = jax.random.uniform(tilt_key, (4, ROWS, COLS), jnp.float32, -1.0, 1.0)
    amplitude = jnp.exp(jax.random.uniform(amp_key, (4, ROWS, COLS), jnp.float32, jnp.log(0.3), 0.0))
    loads = jax.random.uniform(load_key, (CLASSES, ROWS, COLS), jnp.float32, 0.55, 1.0)
    tilt = jnp.repeat(block_tilt, CLASSES // 4, axis=0)
    scale = jnp.repeat(amplitude, CLASSES // 4, axis=0)
    gate = jax.nn.sigmoid(8.0 * tilt * (slot_level[:, None, None] - 0.5))
    return 0.9 * loads * scale * gate


def place_ends(array, key, smallest, high):
    extent = array.shape
    place = [jax.random.randint(jax.random.fold_in(key, axis), (), 0, extent[axis]) for axis in range(len(extent))]
    array = array.at[tuple(place)].set(smallest)
    longest = extent.index(max(extent))
    place[longest] = (place[longest] + 1) % extent[longest]
    return array.at[tuple(place)].set(high)


def steps_of(key, dims, shards, least, top_value):
    def one(position, parts):
        draws = jax.random.uniform(jax.random.fold_in(jax.random.fold_in(key, 6), position), (parts,), jnp.float32, least / len(shards), top_value / len(shards))
        return jnp.repeat(jnp.exp(draws), dims[position] // parts).reshape((-1,) + (1,) * (len(dims) - position - 1))

    factor_of = one(*shards[0])
    for cut in shards[1:]:
        factor_of = factor_of * one(*cut)
    return factor_of


def setup_inputs(seed: int = 0) -> dict:
    streams_of = jax.random.split(jax.random.key(seed), 8)
    return {
        "concentration": draw_concentration(jax.random.fold_in(streams_of[7], 71), 0),
        "class_table": draw_class_table(jax.random.fold_in(streams_of[7], 71), 0),
        "settle_speed": draw_settle_speed(jax.random.fold_in(streams_of[7], 71), 0),
        "along_speed": jnp.clip(0.2 + 0.8 * jax.random.uniform(streams_of[3], (ROWS, COLS), jnp.float32) ** steps_of(streams_of[3], (ROWS, COLS), ((0, 32), (1, 4)), -0.2, 0.2), 0.2, 1.0),
        "across_speed": jnp.clip(jax.random.uniform(streams_of[4], (ROWS, COLS), jnp.float32, -0.5, 0.5) * steps_of(streams_of[4], (ROWS, COLS), ((0, 32), (1, 4)), -0.4, 0.0), -0.5, 0.5),
        "film_depth": jnp.clip(jnp.exp(math.log(2.0) - 1.3862944 * jax.random.uniform(streams_of[5], (ROWS, COLS), jnp.float32) ** steps_of(streams_of[5], (ROWS, COLS), ((0, 32), (1, 4)), -0.2, 0.2)), 0.5, 2.0),
        "cell_mask": place_ends(jax.random.randint(streams_of[6], (ROWS, COLS), 0, 3), jax.random.fold_in(streams_of[6], 1), 0, 2).astype(jnp.int32),
    }


TIME_STEP = 0.25
DIFFUSION = 0.1
VOLUME_PER_UNIT = 0.01
EXPONENT = 4.65


def tendency(extended, speeds, hindrance):
    local_classes = speeds.shape[0]
    fields = extended[:local_classes]
    along = extended[local_classes]
    across = extended[local_classes + 1]
    wetted = extended[local_classes + 2]
    bed_rate = extended[local_classes + 3]
    lower_cells = fields[:, :-1, 1:-1]
    upper_cells = fields[:, 1:, 1:-1]
    face_speed = 0.5 * (along[:-1, 1:-1] + along[1:, 1:-1])
    opening = wetted[:-1, 1:-1] * wetted[1:, 1:-1]
    flux_rows = opening * (jnp.maximum(face_speed, 0.0) * lower_cells + jnp.minimum(face_speed, 0.0) * upper_cells - DIFFUSION * (upper_cells - lower_cells))
    divergence = flux_rows[:, 1:] - flux_rows[:, :-1]
    lower_cells = fields[:, 1:-1, :-1]
    upper_cells = fields[:, 1:-1, 1:]
    face_speed = 0.5 * (across[1:-1, :-1] + across[1:-1, 1:])
    opening = wetted[1:-1, :-1] * wetted[1:-1, 1:]
    flux_cols = opening * (jnp.maximum(face_speed, 0.0) * lower_cells + jnp.minimum(face_speed, 0.0) * upper_cells - DIFFUSION * (upper_cells - lower_cells))
    divergence = divergence + flux_cols[:, :, 1:] - flux_cols[:, :, :-1]
    centre = fields[:, 1:-1, 1:-1]
    settle = speeds[:, None, None] * (hindrance * bed_rate[1:-1, 1:-1])[None] * centre
    return -divergence - settle


def extend(field):
    field = jnp.concatenate([field[:, -1:], field, field[:, :1]], axis=1)
    return jnp.pad(field, ((0, 0), (0, 0), (1, 1)))


def reference(concentration, class_table, settle_speed, along_speed, across_speed, film_depth, cell_mask):
    slot_speed = settle_speed[class_table]
    wetted = (cell_mask > 0).astype(jnp.float32)
    bed_rate = (cell_mask == 2).astype(jnp.float32) / film_depth
    static_ext = extend(jnp.stack([along_speed, across_speed, wetted, bed_rate]))

    def section(fields):
        solids = jnp.sum(fields, axis=0)
        hindrance = (1.0 - VOLUME_PER_UNIT * solids) ** EXPONENT
        groups = fields.reshape(CLASSES // 8, 8, ROWS, COLS)
        speed_groups = slot_speed.reshape(CLASSES // 8, 8)

        def advance(packed):
            group_conc, speeds = packed
            joined = jnp.concatenate([extend(group_conc), static_ext], axis=0)
            return group_conc + TIME_STEP * tendency(joined, speeds, hindrance)

        return lax.map(advance, (groups, speed_groups)).reshape(CLASSES, ROWS, COLS)

    section_one = section(concentration)
    section_two = section(section_one)
    return 0.5 * concentration + 0.5 * section_two
```

```python
import jax
import jax.numpy as jnp
from jax import lax
from jax.experimental import pallas as pl
from jax.experimental.pallas import tpu as pltpu
from jax.sharding import PartitionSpec as P

TIME_STEP = 0.25
DIFFUSION = 0.1
VOLUME_PER_UNIT = 0.01
EXPONENT = 4.65

MESH = pl.DeviceIdType.MESH
SUB, LANE = 8, 128
ALONG, ACROSS, WETTED = 0, 1, 2


def hindered(solids):
    return jnp.exp(EXPONENT * jnp.log(1.0 - VOLUME_PER_UNIT * solids))


def section_kernel(
    conc,
    table,
    settle,
    along,
    across,
    depth,
    mask,
    out,
    field,
    first,
    total,
    partial,
    sibling,
    remote,
    bed,
    coef,
    gain,
    moved,
    depth_v,
    mask_v,
    pack,
    load_sem,
    out_sem,
    send_sem,
    recv_sem,
):
    classes, rows, cols = conc.shape
    row_tiles, col_tiles = rows // SUB, cols // LANE
    helix, cross, cls = lax.axis_index("helix"), lax.axis_index("cross"), lax.axis_index("cls")
    n_helix, n_cross = lax.axis_size("helix"), lax.axis_size("cross")
    core, half = cls % 2, cls // 2
    me_sibling = (helix, cross, half * 2 + 1 - core)
    me_partner = (helix, cross, (1 - half) * 2 + core)
    me_prev = ((helix + n_helix - 1) % n_helix, cross, cls)
    me_next = ((helix + 1) % n_helix, cross, cls)
    me_left = (helix, (cross + n_cross - 1) % n_cross, cls)
    me_right = (helix, (cross + 1) % n_cross, cls)

    inner_cols = pl.ds(LANE, cols)

    loads = []
    for r in range(row_tiles):
        loads.append(
            pltpu.make_async_copy(
                conc.at[:, pl.ds(r * SUB, SUB), :],
                field.at[pl.ds(0, classes), pl.ds(SUB + r * SUB, SUB), inner_cols],
                load_sem.at[r],
            )
        )
    statics = [
        pltpu.make_async_copy(
            along, field.at[classes + ALONG, pl.ds(SUB, rows), inner_cols], load_sem.at[row_tiles]
        ),
        pltpu.make_async_copy(
            across, field.at[classes + ACROSS, pl.ds(SUB, rows), inner_cols], load_sem.at[row_tiles + 1]
        ),
        pltpu.make_async_copy(depth, depth_v, load_sem.at[row_tiles + 2]),
        pltpu.make_async_copy(mask, mask_v, load_sem.at[row_tiles + 3]),
    ]
    for copy in loads + statics:
        copy.start()

    barrier = pltpu.get_barrier_semaphore()
    peers = (me_sibling, me_partner, me_prev, me_next, me_left, me_right)
    for peer in peers:
        pl.semaphore_signal(barrier, inc=1, device_id=peer, device_id_type=MESH)

    speed = [settle[table[k]] for k in range(classes)]
    sub = lax.broadcasted_iota(jnp.int32, (SUB, LANE), 0)
    lane = lax.broadcasted_iota(jnp.int32, (SUB, LANE), 1)

    def tile(ref, plane, r, j):
        return ref[
            plane,
            pl.ds(pl.multiple_of(SUB + r * SUB, SUB), SUB),
            pl.ds(pl.multiple_of(LANE + j * LANE, LANE), LANE),
        ]

    def put(ref, plane, r, j, value):
        ref[
            plane,
            pl.ds(pl.multiple_of(SUB + r * SUB, SUB), SUB),
            pl.ds(pl.multiple_of(LANE + j * LANE, LANE), LANE),
        ] = value

    def at(r, j):
        return pl.ds(pl.multiple_of(r * SUB, SUB), SUB), pl.ds(pl.multiple_of(j * LANE, LANE), LANE)

    def north(ref, plane, r, j, x):
        return pltpu.roll(jnp.where(sub == SUB - 1, tile(ref, plane, r - 1, j), x), 1, 0)

    def south(ref, plane, r, j, x):
        return pltpu.roll(jnp.where(sub == 0, tile(ref, plane, r + 1, j), x), SUB - 1, 0)

    def west(ref, plane, r, j, x):
        return pltpu.roll(jnp.where(lane == LANE - 1, tile(ref, plane, r, j - 1), x), 1, 1)

    def east(ref, plane, r, j, x):
        return pltpu.roll(jnp.where(lane == 0, tile(ref, plane, r, j + 1), x), LANE - 1, 1)

    def over_cols(body):
        def step(j, carry):
            body(j)
            return carry

        lax.fori_loop(0, col_tiles, step, 0)

    def over_tiles(body, tiles):
        def step(i, carry):
            body(tiles[0] + i // col_tiles * tiles[1], i % col_tiles)
            return carry

        lax.fori_loop(0, tiles[2] * col_tiles, step, 0)

    for r in range(row_tiles):
        loads[r].wait()

        def sums(j):
            parts_s, parts_w = [], []
            for k in range(classes):
                x = tile(field, k, r, j)
                parts_s.append(x)
                parts_w.append(speed[k] * x)
            while len(parts_s) > 1:
                parts_s = [a + b for a, b in zip(parts_s[::2], parts_s[1::2])]
                parts_w = [a + b for a, b in zip(parts_w[::2], parts_w[1::2])]
            partial[(0, *at(r, j))] = parts_s[0]
            partial[(1, *at(r, j))] = parts_w[0]

        over_cols(sums)

    for copy in statics:
        copy.wait()

    def statics_of(r, j):
        kind = mask_v[at(r, j)]
        put(field, classes + WETTED, r, j, (kind > 0).astype(jnp.float32))
        bed[at(r, j)] = jnp.where(kind == 2, TIME_STEP, 0.0) / depth_v[at(r, j)]

    over_tiles(statics_of, (0, 1, row_tiles))

    def pack_cols(ref, planes, slot):
        for r in range(row_tiles):
            head = jnp.zeros((SUB, LANE), jnp.float32)
            tail = jnp.zeros((SUB, LANE), jnp.float32)
            for p in range(planes):
                x = tile(ref, p, r, 0)
                head = jnp.where(lane == p, pltpu.roll(x, p, 1) if p else x, head)
                x = tile(ref, p, r, col_tiles - 1)
                tail = jnp.where(lane == p, pltpu.roll(x, p + 1, 1), tail)
            pack[(slot, *at(r, 0))] = head
            pack[(slot + 1, *at(r, 0))] = tail

    def unpack_cols(ref, planes, slot, walls):
        for r in range(row_tiles):
            head = pack[(slot + 2, *at(r, 0))]
            tail = pack[(slot + 3, *at(r, 0))]
            for p in range(planes):
                right = pltpu.roll(head, LANE - p, 1) if p else head
                left = pltpu.roll(tail, LANE - 1 - p, 1)
                if p in walls:
                    right = jnp.where(cross < n_cross - 1, right, 0.0)
                    left = jnp.where(cross > 0, left, 0.0)
                put(ref, p, r, col_tiles, right)
                put(ref, p, r, -1, left)

    pack_cols(field, classes + 3, 0)

    def send(index, src, dst, peer):
        copy = pltpu.make_async_remote_copy(
            src_ref=src,
            dst_ref=dst,
            send_sem=send_sem.at[index],
            recv_sem=recv_sem.at[index],
            device_id=peer,
            device_id_type=MESH,
        )
        copy.start()
        return copy

    pl.semaphore_wait(barrier, len(peers))

    shares = [send(q, partial.at[q], sibling.at[q], me_sibling) for q in range(2)]

    def send_halos(index, ref, planes, slot):
        every = pl.ds(0, planes)
        return [
            send(index, ref.at[every, pl.ds(SUB + rows - 1, 1), inner_cols], ref.at[every, pl.ds(SUB - 1, 1), inner_cols], me_next),
            send(index + 1, ref.at[every, pl.ds(SUB, 1), inner_cols], ref.at[every, pl.ds(SUB + rows, 1), inner_cols], me_prev),
        ]

    def send_cols(index, slot):
        return [
            send(index, pack.at[slot], pack.at[slot + 2], me_left),
            send(index + 1, pack.at[slot + 1], pack.at[slot + 3], me_right),
        ]

    def own_rows(t):
        return pl.ds(pl.multiple_of(SUB * (t + core * (row_tiles - 1 - 2 * t)), SUB), SUB)

    def other_rows(t):
        return pl.ds(pl.multiple_of(SUB * (t + (1 - core) * (row_tiles - 1 - 2 * t)), SUB), SUB)

    steps = row_tiles // 2
    far = []
    for q in range(2):
        shares[q].wait()
        for t in range(steps):
            own = own_rows(t)
            partial_sum = partial[q, own, :] + sibling[q, own, :]
            total[q, own, :] = partial_sum
            far.append(send(2 + q * steps + t, total.at[q, own, :], remote.at[q, own, :], me_partner))
        for t in range(steps):
            other = other_rows(t)
            total[q, other, :] = partial[q, other, :] + sibling[q, other, :]
    base = 2 + 2 * steps
    row_halo = send_halos(base, field, classes + 3, 0)
    col_halo = send_cols(base + 2, 0)

    for copy in col_halo + row_halo:
        copy.wait_recv()
    unpack_cols(field, classes + 3, 0, (classes + WETTED,))

    def coefficients(r, j):
        u = tile(field, classes + ALONG, r, j)
        v = tile(field, classes + ACROSS, r, j)
        w = tile(field, classes + WETTED, r, j)

        def face(speed_a, speed_b, wet_b):
            face_speed = 0.5 * (speed_a + speed_b)
            opening = TIME_STEP * (w * wet_b)
            ahead = opening * (jnp.maximum(face_speed, 0.0) + DIFFUSION)
            back = opening * (DIFFUSION - jnp.minimum(face_speed, 0.0))
            return ahead, back

        wet = classes + WETTED
        from_north, to_north = face(u, north(field, classes + ALONG, r, j, u), north(field, wet, r, j, w))
        to_south, from_south = face(u, south(field, classes + ALONG, r, j, u), south(field, wet, r, j, w))
        from_west, to_west = face(v, west(field, classes + ACROSS, r, j, v), west(field, wet, r, j, w))
        to_east, from_east = face(v, east(field, classes + ACROSS, r, j, v), east(field, wet, r, j, w))
        coef[(0, *at(r, j))] = from_north
        coef[(1, *at(r, j))] = from_south
        coef[(2, *at(r, j))] = from_west
        coef[(3, *at(r, j))] = from_east
        coef[(4, *at(r, j))] = 1.0 - ((to_north + to_south) + (to_west + to_east))

    over_tiles(coefficients, (0, 1, row_tiles))

    def transported(ref, plane, r, j, factors):
        x = tile(ref, plane, r, j)
        along_part = factors[0] * north(ref, plane, r, j, x) + factors[1] * south(ref, plane, r, j, x)
        across_part = factors[2] * west(ref, plane, r, j, x) + factors[3] * east(ref, plane, r, j, x)
        return factors[4] * x + (along_part + across_part)

    def carry_first(r, j):
        factors = [coef[(i, *at(r, j))] for i in range(5)]
        for k in range(classes):
            put(first, k, r, j, transported(field, k, r, j, factors))

    over_tiles(carry_first, (0, 1, row_tiles))

    def receive(q, t):
        far[q * steps + t].wait_recv()
        own = own_rows(t)
        return send(base + 8 + q * steps + t, remote.at[q, own, :], remote.at[q, own, :], me_sibling)

    def arrived(q, t):
        pltpu.make_async_remote_copy(
            src_ref=remote.at[q, other_rows(t), :],
            dst_ref=remote.at[q, other_rows(t), :],
            send_sem=send_sem.at[base + 8 + q * steps + t],
            recv_sem=recv_sem.at[base + 8 + q * steps + t],
            device_id=me_sibling,
            device_id_type=MESH,
        ).wait_recv()

    forwards = []

    def section_one(r, j):
        solids = total[(0, *at(r, j))] + remote[(0, *at(r, j))]
        put(first, classes, r, j, solids)
        g = bed[at(r, j)] * hindered(solids)
        gain[at(r, j)] = g
        for k in range(classes):
            put(first, k, r, j, tile(first, k, r, j) - (speed[k] * g) * tile(field, k, r, j))

    halos = None
    for t in range(steps):
        forwards.append(receive(0, t))
        arrived(0, t)
        over_tiles(section_one, (t, row_tiles - 1 - 2 * t, 2))
        if t == 0:
            row_halo_one = send_halos(base + 4, first, classes + 1, 4)
    pack_cols(first, classes + 1, 4)
    col_halo_one = send_cols(base + 6, 4)

    def carry_second(r, j):
        factors = [coef[(i, *at(r, j))] for i in range(5)]
        for k in range(classes):
            value = tile(field, k, r, j) + transported(first, k, r, j, factors)
            moved[(k, *at(r, j))] = 0.5 * value
        moved[(classes, *at(r, j))] = transported(first, classes, r, j, factors)

    for copy in col_halo_one:
        copy.wait_recv()
    unpack_cols(first, classes + 1, 4, ())
    over_tiles(carry_second, (1, 1, row_tiles - 2))
    for copy in row_halo_one:
        copy.wait_recv()
    over_tiles(carry_second, (0, row_tiles - 1, 2))

    def finish(r, j):
        weighted = total[(1, *at(r, j))] + remote[(1, *at(r, j))]
        solids = moved[(classes, *at(r, j))] - gain[at(r, j)] * weighted
        g = (0.5 * bed[at(r, j)]) * hindered(solids)
        for k in range(classes):
            moved[(k, *at(r, j))] = moved[(k, *at(r, j))] - (speed[k] * g) * tile(first, k, r, j)

    stores = []
    for t in range(steps):
        forwards.append(receive(1, t))
        arrived(1, t)
        over_tiles(finish, (t, row_tiles - 1 - 2 * t, 2))
        for r in (t, row_tiles - 1 - t):
            copy = pltpu.make_async_copy(
                moved.at[pl.ds(0, classes), pl.ds(r * SUB, SUB), :],
                out.at[:, pl.ds(r * SUB, SUB), :],
                out_sem.at[r],
            )
            copy.start()
            stores.append(copy)

    for copy in shares:
        pass
    for copy in far + row_halo + col_halo + forwards + row_halo_one + col_halo_one:
        copy.wait_send()
    for copy in stores:
        copy.wait()


def per_device(concentration, class_table, settle_speed, along_speed, across_speed, film_depth, cell_mask):
    classes, rows, cols = concentration.shape
    padded = (rows + 2 * SUB, cols + 2 * LANE)
    flat = (rows, cols)
    row_tiles = rows // SUB
    copies = 2 + 4 * (row_tiles // 2) + 8
    anywhere = pl.BlockSpec(memory_space=pl.ANY)
    scalars = pl.BlockSpec(memory_space=pltpu.SMEM)
    f32 = jnp.float32
    return pl.pallas_call(
        section_kernel,
        out_shape=jax.ShapeDtypeStruct(concentration.shape, f32),
        in_specs=[anywhere, scalars, scalars, anywhere, anywhere, anywhere, anywhere],
        out_specs=anywhere,
        scratch_shapes=[
            pltpu.VMEM((classes + 3, *padded), f32),
            pltpu.VMEM((classes + 1, *padded), f32),
            pltpu.VMEM((2, *flat), f32),
            pltpu.VMEM((2, *flat), f32),
            pltpu.VMEM((2, *flat), f32),
            pltpu.VMEM((2, *flat), f32),
            pltpu.VMEM(flat, f32),
            pltpu.VMEM((5, *flat), f32),
            pltpu.VMEM(flat, f32),
            pltpu.VMEM((classes + 1, *flat), f32),
            pltpu.VMEM(flat, f32),
            pltpu.VMEM(flat, jnp.int32),
            pltpu.VMEM((8, rows, LANE), f32),
            pltpu.SemaphoreType.DMA((row_tiles + 4,)),
            pltpu.SemaphoreType.DMA((row_tiles,)),
            pltpu.SemaphoreType.DMA((copies,)),
            pltpu.SemaphoreType.DMA((copies,)),
        ],
        compiler_params=pltpu.CompilerParams(
            collective_id=0, has_side_effects=True, vmem_limit_bytes=32 * 2**20
        ),
        cost_estimate=pl.CostEstimate(
            flops=40 * classes * rows * cols, bytes_accessed=8 * classes * rows * cols, transcendentals=4 * rows * cols
        ),
    )(concentration, class_table, settle_speed, along_speed, across_speed, film_depth, cell_mask)


def solution(mesh):
    grid = P("helix", "cross")
    return jax.shard_map(
        per_device,
        mesh=mesh,
        in_specs=(P("cls", "helix", "cross"), P("cls"), P(), grid, grid, grid, grid),
        out_specs=P("cls", "helix", "cross"),
        check_vma=False,
    )
```

```python
import jax
import jax.numpy as jnp
from jax import lax
from jax.experimental import pallas as pl
from jax.experimental.pallas import tpu as pltpu
from jax.sharding import PartitionSpec as P

TIME_STEP = 0.25
DIFFUSION = 0.1
VOLUME_PER_UNIT = 0.01
EXPONENT = 4.65

MESH = pl.DeviceIdType.MESH
SUB, LANE = 8, 128
ALONG, ACROSS, WETTED, BED = 0, 1, 2, 3


def hindered(solids):
    return jnp.exp(EXPONENT * jnp.log(1.0 - VOLUME_PER_UNIT * solids))


def section_kernel(
    conc,
    table,
    settle,
    along,
    across,
    depth,
    mask,
    out,
    table_s,
    settle_s,
    field,
    first,
    edges,
    total,
    partial,
    sibling,
    remote,
    coef,
    gain,
    moved,
    depth_v,
    mask_v,
    pack,
    corner,
    load_sem,
    send_sem,
    recv_sem,
):
    classes, rows, cols = conc.shape
    row_tiles, col_tiles = rows // SUB, cols // LANE
    helix, cross, cls = lax.axis_index("helix"), lax.axis_index("cross"), lax.axis_index("cls")
    n_helix, n_cross = lax.axis_size("helix"), lax.axis_size("cross")
    core, half = cls % 2, cls // 2
    me_sibling = (helix, cross, half * 2 + 1 - core)
    me_partner = (helix, cross, (1 - half) * 2 + core)
    me_prev = ((helix + n_helix - 1) % n_helix, cross, cls)
    me_next = ((helix + 1) % n_helix, cross, cls)
    far_prev = ((helix + n_helix - 1) % n_helix, cross, (1 - half) * 2 + core)
    far_next = ((helix + 1) % n_helix, cross, (1 - half) * 2 + core)
    me_left = (helix, (cross + n_cross - 1) % n_cross, cls)
    me_right = (helix, (cross + 1) % n_cross, cls)

    inner_cols = pl.ds(LANE, cols)
    last = row_tiles - 1
    steps = row_tiles // 2
    planes = classes + 4

    loads = [
        pltpu.make_async_copy(
            conc.at[:, pl.ds(r * SUB, SUB), :],
            field.at[pl.ds(0, classes), pl.ds(SUB + r * SUB, SUB), inner_cols],
            load_sem.at[r],
        )
        for r in range(row_tiles)
    ]
    scalars = [
        pltpu.make_async_copy(table, table_s, load_sem.at[row_tiles + 4]),
        pltpu.make_async_copy(settle, settle_s, load_sem.at[row_tiles + 5]),
    ]
    inner = pl.ds(SUB, rows)
    statics = [
        pltpu.make_async_copy(along, field.at[classes + ALONG, inner, inner_cols], load_sem.at[row_tiles]),
        pltpu.make_async_copy(across, field.at[classes + ACROSS, inner, inner_cols], load_sem.at[row_tiles + 1]),
        pltpu.make_async_copy(depth, depth_v, load_sem.at[row_tiles + 2]),
        pltpu.make_async_copy(mask, mask_v, load_sem.at[row_tiles + 3]),
    ]
    for copy in scalars + loads + statics:
        copy.start()

    barrier = pltpu.get_barrier_semaphore()
    peers = (me_sibling, me_partner, me_prev, me_next, far_prev, far_next, me_left, me_right)
    for peer in peers:
        pl.semaphore_signal(barrier, inc=1, device_id=peer, device_id_type=MESH)

    for copy in scalars:
        copy.wait()
    speed = [settle_s[table_s[k]] for k in range(classes)]
    sub = lax.broadcasted_iota(jnp.int32, (SUB, LANE), 0)
    lane = lax.broadcasted_iota(jnp.int32, (SUB, LANE), 1)

    def at(r, j):
        return pl.ds(pl.multiple_of(r * SUB, SUB), SUB), pl.ds(pl.multiple_of(j * LANE, LANE), LANE)

    def tile(ref, plane, r, j):
        return ref[(plane, *at(r + 1, j + 1))]

    def put(ref, plane, r, j, value):
        ref[(plane, *at(r + 1, j + 1))] = value

    def north(ref, plane, r, j, x, side=0):
        if side >= 0:
            x = jnp.where(sub == SUB - 1, tile(ref, plane, r - 1, j), x)
        return pltpu.roll(x, 1, 0)

    def south(ref, plane, r, j, x, side=0):
        if side <= 0:
            x = jnp.where(sub == 0, tile(ref, plane, r + 1, j), x)
        return pltpu.roll(x, SUB - 1, 0)

    def west(ref, plane, r, j, x):
        return pltpu.roll(jnp.where(lane == LANE - 1, tile(ref, plane, r, j - 1), x), 1, 1)

    def east(ref, plane, r, j, x):
        return pltpu.roll(jnp.where(lane == 0, tile(ref, plane, r, j + 1), x), LANE - 1, 1)

    def over(body, r0, rstep, nr, j0=0, jstep=1, nj=col_tiles, unroll=4):
        def step(i, carry):
            body(r0 + i // nj * rstep, j0 + i % nj * jstep)
            return carry

        lax.fori_loop(0, nr * nj, step, 0, unroll=unroll)

    def sums(r, j):
        parts_s, parts_w = [], []
        for k in range(classes):
            x = tile(field, k, r, j)
            parts_s.append(x)
            parts_w.append(speed[k] * x)
        while len(parts_s) > 1:
            parts_s = [a + b for a, b in zip(parts_s[::2], parts_s[1::2])]
            parts_w = [a + b for a, b in zip(parts_w[::2], parts_w[1::2])]
        partial[(0, *at(r, j))] = parts_s[0]
        partial[(1, *at(r, j))] = parts_w[0]

    for r in range(row_tiles):
        loads[r].wait()
        over(sums, r, 1, 1, unroll=2)

    used = []

    def send(src, dst, peer):
        index = len(used)
        used.append(index)
        copy = pltpu.make_async_remote_copy(
            src_ref=src,
            dst_ref=dst,
            send_sem=send_sem.at[index],
            recv_sem=recv_sem.at[index],
            device_id=peer,
            device_id_type=MESH,
        )
        copy.start()
        return copy

    pl.semaphore_wait(barrier, len(peers))

    shares = [send(partial.at[0], sibling.at[0], me_sibling)]

    def send_rows(start, count):
        some = pl.ds(start, count)
        return [
            send(
                field.at[some, pl.ds(SUB + rows - 2, 2), inner_cols],
                field.at[some, pl.ds(SUB - 2, 2), inner_cols],
                me_next,
            ),
            send(
                field.at[some, pl.ds(SUB, 2), inner_cols],
                field.at[some, pl.ds(SUB + rows, 2), inner_cols],
                me_prev,
            ),
        ]

    row_halo = send_rows(0, classes)
    shares.append(send(partial.at[1], sibling.at[1], me_sibling))

    for copy in statics:
        copy.wait()

    def statics_of(r, j):
        kind = mask_v[at(r, j)]
        put(field, classes + WETTED, r, j, (kind > 0).astype(jnp.float32))
        put(field, classes + BED, r, j, jnp.where(kind == 2, TIME_STEP, 0.0) / depth_v[at(r, j)])

    def own_rows(t):
        return pl.ds(pl.multiple_of(SUB * (t + core * (last - 2 * t)), SUB), SUB)

    def other_rows(t):
        return pl.ds(pl.multiple_of(SUB * (t + (1 - core) * (last - 2 * t)), SUB), SUB)

    far = []

    def chip_sums(q):
        shares[q].wait()
        for t in range(steps):
            own = own_rows(t)
            total[q, own, :] = partial[q, own, :] + sibling[q, own, :]
            far.append(send(total.at[q, own, :], remote.at[q, own, :], me_partner))
        for t in range(steps):
            other = other_rows(t)
            total[q, other, :] = partial[q, other, :] + sibling[q, other, :]

    chip_sums(0)
    edge_sums = []
    for source, after, before in ((0, me_next, me_prev), (1, far_next, far_prev)):
        edge_sums.append(
            send(total.at[0, pl.ds(rows - 1, 1), :], edges.at[source, 0, pl.ds(SUB - 1, 1), :], after)
        )
        edge_sums.append(send(total.at[0, pl.ds(0, 1), :], edges.at[source, 1, pl.ds(0, 1), :], before))

    over(statics_of, 0, 1, row_tiles)
    row_halo += send_rows(classes, 4)

    def pack_cols(ref, count, dst, slot, tile_rows):
        for i, r in enumerate(tile_rows):
            head = jnp.zeros((SUB, LANE), jnp.float32)
            tail = jnp.zeros((SUB, LANE), jnp.float32)
            for p in range(count):
                x = tile(ref, p, r, 0)
                head = jnp.where(lane == p, pltpu.roll(x, p, 1) if p else x, head)
                x = tile(ref, p, r, col_tiles - 1)
                tail = jnp.where(lane == p, pltpu.roll(x, p + 1, 1), tail)
            dst[(slot, *at(i, 0))] = head
            dst[(slot + 1, *at(i, 0))] = tail

    def send_cols(src, slot):
        return [
            send(src.at[slot], src.at[slot + 2], me_left),
            send(src.at[slot + 1], src.at[slot + 3], me_right),
        ]

    def unpack_cols(ref, count, src, slot, tile_rows, walls):
        for i, r in enumerate(tile_rows):
            head = src[(slot + 2, *at(i, 0))]
            tail = src[(slot + 3, *at(i, 0))]
            for p in range(count):
                right = pltpu.roll(head, LANE - p, 1) if p else head
                left = pltpu.roll(tail, LANE - 1 - p, 1)
                if p in walls:
                    right = jnp.where(cross < n_cross - 1, right, 0.0)
                    left = jnp.where(cross > 0, left, 0.0)
                put(ref, p, r, col_tiles, right)
                put(ref, p, r, -1, left)

    own_tiles = tuple(range(row_tiles))
    outer_tiles = (-1, row_tiles)
    walls = (classes + WETTED,)

    pack_cols(field, classes + 3, pack, 0, own_tiles)
    col_halo = send_cols(pack, 0)
    chip_sums(1)

    def coefficients(r, j, side=0):
        u = tile(field, classes + ALONG, r, j)
        v = tile(field, classes + ACROSS, r, j)
        w = tile(field, classes + WETTED, r, j)

        def face(speed_a, speed_b, wet_b):
            face_speed = 0.5 * (speed_a + speed_b)
            opening = TIME_STEP * (w * wet_b)
            ahead = opening * (jnp.maximum(face_speed, 0.0) + DIFFUSION)
            back = opening * (DIFFUSION - jnp.minimum(face_speed, 0.0))
            return ahead, back

        wet = classes + WETTED
        speed_plane = classes + ALONG
        from_north, to_north = face(
            u, north(field, speed_plane, r, j, u, side), north(field, wet, r, j, w, side)
        )
        to_south, from_south = face(
            u, south(field, speed_plane, r, j, u, side), south(field, wet, r, j, w, side)
        )
        from_west, to_west = face(v, west(field, classes + ACROSS, r, j, v), west(field, wet, r, j, w))
        to_east, from_east = face(v, east(field, classes + ACROSS, r, j, v), east(field, wet, r, j, w))
        coef[(0, *at(r + 1, j))] = from_north
        coef[(1, *at(r + 1, j))] = from_south
        coef[(2, *at(r + 1, j))] = from_west
        coef[(3, *at(r + 1, j))] = from_east
        coef[(4, *at(r + 1, j))] = 1.0 - ((to_north + to_south) + (to_west + to_east))

    def transported(ref, plane, r, j, factors, side=0):
        x = tile(ref, plane, r, j)
        along_part = factors[0] * north(ref, plane, r, j, x, side) + factors[1] * south(ref, plane, r, j, x, side)
        across_part = factors[2] * west(ref, plane, r, j, x) + factors[3] * east(ref, plane, r, j, x)
        return factors[4] * x + (along_part + across_part)

    def carry_first(r, j, side=0):
        factors = [coef[(i, *at(r + 1, j))] for i in range(5)]
        for k in range(classes):
            put(first, k, r, j, transported(field, k, r, j, factors, side))

    for copy in col_halo:
        copy.wait_recv()
    unpack_cols(field, classes + 3, pack, 0, own_tiles, walls)
    over(coefficients, 1, 1, row_tiles - 2)
    over(carry_first, 1, 1, row_tiles - 2)

    for copy in row_halo:
        copy.wait_recv()
    pack_cols(field, classes + 3, corner, 0, outer_tiles)
    corners = send_cols(corner, 0)
    over(coefficients, 0, last, 2)
    over(carry_first, 0, last, 2)
    for copy in corners:
        copy.wait_recv()
    unpack_cols(field, classes + 3, corner, 0, outer_tiles, walls)

    def section_one(r, j, solids, keep_gain):
        put(first, classes, r, j, solids)
        g = tile(field, classes + BED, r, j) * hindered(solids)
        if keep_gain:
            gain[at(r, j)] = g
        for k in range(classes):
            put(first, k, r, j, tile(first, k, r, j) - (speed[k] * g) * tile(field, k, r, j))

    for copy in edge_sums:
        copy.wait_recv()
    for side, r in ((-1, -1), (1, row_tiles)):

        def outer(_, j, side=side, r=r):
            coefficients(r, j, side)
            carry_first(r, j, side)
            low = 0 if side < 0 else 1
            strip = pl.ds(pl.multiple_of(j * LANE, LANE), LANE)
            section_one(r, j, edges[0, low, :, strip] + edges[1, low, :, strip], False)

        over(outer, r, 1, 1, unroll=2)

    forwards = []

    def receive(q, t):
        far[q * steps + t].wait_recv()
        own, other = own_rows(t), other_rows(t)
        forward = send(remote.at[q, own, :], remote.at[q, own, :], me_sibling)
        forwards.append(forward)
        index = used[-1]
        pltpu.make_async_remote_copy(
            src_ref=remote.at[q, other, :],
            dst_ref=remote.at[q, other, :],
            send_sem=send_sem.at[index],
            recv_sem=recv_sem.at[index],
            device_id=me_sibling,
            device_id_type=MESH,
        ).wait_recv()

    def section_one_own(r, j):
        section_one(r, j, total[(0, *at(r, j))] + remote[(0, *at(r, j))], True)

    for t in range(steps):
        receive(0, t)
        over(section_one_own, t, last - 2 * t, 2)
    pack_cols(first, classes + 1, pack, 4, own_tiles)
    col_halo_one = send_cols(pack, 4)

    def carry_second(r, j):
        factors = [coef[(i, *at(r + 1, j))] for i in range(5)]
        for k in range(classes):
            value = tile(field, k, r, j) + transported(first, k, r, j, factors)
            out[(k, *at(r, j))] = 0.5 * value
        moved[at(r, j)] = transported(first, classes, r, j, factors)

    over(carry_second, 0, 1, row_tiles, 1, 1, col_tiles - 2)
    for copy in col_halo_one:
        copy.wait_recv()
    unpack_cols(first, classes + 1, pack, 4, own_tiles, ())
    over(carry_second, 0, 1, row_tiles, 0, col_tiles - 1, 2)

    def finish(r, j):
        weighted = total[(1, *at(r, j))] + remote[(1, *at(r, j))]
        solids = moved[at(r, j)] - gain[at(r, j)] * weighted
        g = (0.5 * tile(field, classes + BED, r, j)) * hindered(solids)
        for k in range(classes):
            out[(k, *at(r, j))] = out[(k, *at(r, j))] - (speed[k] * g) * tile(first, k, r, j)

    for t in range(steps):
        receive(1, t)
        over(finish, t, last - 2 * t, 2)

    for copy in far + edge_sums + row_halo + col_halo + corners + forwards + col_halo_one:
        copy.wait_send()


def per_device(concentration, class_table, settle_speed, along_speed, across_speed, film_depth, cell_mask):
    classes, rows, cols = concentration.shape
    padded = (rows + 2 * SUB, cols + 2 * LANE)
    flat = (rows, cols)
    row_tiles = rows // SUB
    copies = 2 + 4 * (row_tiles // 2) + 4 + 4 + 6
    anywhere = pl.BlockSpec(memory_space=pl.ANY)
    f32 = jnp.float32

    def keep(array):
        return pltpu.with_memory_space_constraint(array, pltpu.HBM)

    return pl.pallas_call(
        section_kernel,
        out_shape=pltpu.VMEM(concentration.shape, f32),
        in_specs=[anywhere] * 7,
        out_specs=pl.BlockSpec(memory_space=pltpu.VMEM),
        scratch_shapes=[
            pltpu.SMEM(class_table.shape, jnp.int32),
            pltpu.SMEM(settle_speed.shape, f32),
            pltpu.VMEM((classes + 4, *padded), f32),
            pltpu.VMEM((classes + 1, *padded), f32),
            pltpu.VMEM((2, 2, SUB, cols), f32),
            pltpu.VMEM((2, *flat), f32),
            pltpu.VMEM((2, *flat), f32),
            pltpu.VMEM((2, *flat), f32),
            pltpu.VMEM((2, *flat), f32),
            pltpu.VMEM((5, rows + 2 * SUB, cols), f32),
            pltpu.VMEM(flat, f32),
            pltpu.VMEM(flat, f32),
            pltpu.VMEM(flat, f32),
            pltpu.VMEM(flat, jnp.int32),
            pltpu.VMEM((8, rows, LANE), f32),
            pltpu.VMEM((4, 2 * SUB, LANE), f32),
            pltpu.SemaphoreType.DMA((row_tiles + 6,)),
            pltpu.SemaphoreType.DMA((copies,)),
            pltpu.SemaphoreType.DMA((copies,)),
        ],
        compiler_params=pltpu.CompilerParams(
            collective_id=0, has_side_effects=True, vmem_limit_bytes=32 * 2**20
        ),
        cost_estimate=pl.CostEstimate(
            flops=40 * classes * rows * cols, bytes_accessed=8 * classes * rows * cols, transcendentals=4 * rows * cols
        ),
    )(*map(keep, (concentration, class_table, settle_speed, along_speed, across_speed, film_depth, cell_mask)))


def solution(mesh):
    grid = P("helix", "cross")
    return jax.shard_map(
        per_device,
        mesh=mesh,
        in_specs=(P("cls", "helix", "cross"), P("cls"), P(), grid, grid, grid, grid),
        out_specs=P("cls", "helix", "cross"),
        check_vma=False,
    )
```

```python
import jax
import jax.numpy as jnp
from jax import lax
from jax.experimental import pallas as pl
from jax.experimental.pallas import tpu as pltpu
from jax.sharding import PartitionSpec as P

TIME_STEP = 0.25
DIFFUSION = 0.1
VOLUME_PER_UNIT = 0.01
EXPONENT = 4.65

MESH = pl.DeviceIdType.MESH
SUB, LANE = 8, 128
ALONG, ACROSS, WETTED, BED = 0, 1, 2, 3


def hindered(solids):
    return jnp.exp(EXPONENT * jnp.log(1.0 - VOLUME_PER_UNIT * solids))


def section_kernel(
    conc,
    table,
    settle,
    along,
    across,
    depth,
    mask,
    out,
    table_s,
    settle_s,
    field,
    first,
    edges,
    total,
    partial,
    sibling,
    remote,
    coef,
    gain,
    moved,
    depth_v,
    mask_v,
    pack,
    corner,
    load_sem,
    send_sem,
    recv_sem,
):
    classes, rows, cols = conc.shape
    row_tiles, col_tiles = rows // SUB, cols // LANE
    helix, cross, cls = lax.axis_index("helix"), lax.axis_index("cross"), lax.axis_index("cls")
    n_helix, n_cross = lax.axis_size("helix"), lax.axis_size("cross")
    core, half = cls % 2, cls // 2
    me_sibling = (helix, cross, half * 2 + 1 - core)
    me_partner = (helix, cross, (1 - half) * 2 + core)
    me_prev = ((helix + n_helix - 1) % n_helix, cross, cls)
    me_next = ((helix + 1) % n_helix, cross, cls)
    far_prev = ((helix + n_helix - 1) % n_helix, cross, (1 - half) * 2 + core)
    far_next = ((helix + 1) % n_helix, cross, (1 - half) * 2 + core)
    me_left = (helix, (cross + n_cross - 1) % n_cross, cls)
    me_right = (helix, (cross + 1) % n_cross, cls)

    prev_left, prev_right = (me_prev[0], me_left[1], cls), (me_prev[0], me_right[1], cls)
    next_left, next_right = (me_next[0], me_left[1], cls), (me_next[0], me_right[1], cls)

    inner_cols = pl.ds(LANE, cols)
    last = row_tiles - 1
    steps = row_tiles // 2
    planes = classes + 4

    loads = [
        pltpu.make_async_copy(
            conc.at[:, pl.ds(r * SUB, SUB), :],
            field.at[pl.ds(0, classes), pl.ds(SUB + r * SUB, SUB), inner_cols],
            load_sem.at[r],
        )
        for r in range(row_tiles)
    ]
    scalars = [
        pltpu.make_async_copy(table, table_s, load_sem.at[row_tiles + 4]),
        pltpu.make_async_copy(settle, settle_s, load_sem.at[row_tiles + 5]),
    ]
    inner = pl.ds(SUB, rows)
    statics = [
        pltpu.make_async_copy(along, field.at[classes + ALONG, inner, inner_cols], load_sem.at[row_tiles]),
        pltpu.make_async_copy(across, field.at[classes + ACROSS, inner, inner_cols], load_sem.at[row_tiles + 1]),
        pltpu.make_async_copy(depth, depth_v, load_sem.at[row_tiles + 2]),
        pltpu.make_async_copy(mask, mask_v, load_sem.at[row_tiles + 3]),
    ]
    for copy in scalars + loads + statics:
        copy.start()

    barrier = pltpu.get_barrier_semaphore()
    peers = (me_sibling, me_partner, me_prev, me_next, far_prev, far_next, me_left, me_right)
    peers += (prev_left, prev_right, next_left, next_right)
    for peer in peers:
        pl.semaphore_signal(barrier, inc=1, device_id=peer, device_id_type=MESH)

    for copy in scalars:
        copy.wait()
    speed = [settle_s[table_s[k]] for k in range(classes)]
    sub = lax.broadcasted_iota(jnp.int32, (SUB, LANE), 0)
    lane = lax.broadcasted_iota(jnp.int32, (SUB, LANE), 1)

    def at(r, j):
        return pl.ds(pl.multiple_of(r * SUB, SUB), SUB), pl.ds(pl.multiple_of(j * LANE, LANE), LANE)

    def tile(ref, plane, r, j):
        return ref[(plane, *at(r + 1, j + 1))]

    def put(ref, plane, r, j, value):
        ref[(plane, *at(r + 1, j + 1))] = value

    def north(ref, plane, r, j, x, side=0):
        if side >= 0:
            x = jnp.where(sub == SUB - 1, tile(ref, plane, r - 1, j), x)
        return pltpu.roll(x, 1, 0)

    def south(ref, plane, r, j, x, side=0):
        if side <= 0:
            x = jnp.where(sub == 0, tile(ref, plane, r + 1, j), x)
        return pltpu.roll(x, SUB - 1, 0)

    def west(ref, plane, r, j, x):
        return pltpu.roll(jnp.where(lane == LANE - 1, tile(ref, plane, r, j - 1), x), 1, 1)

    def east(ref, plane, r, j, x):
        return pltpu.roll(jnp.where(lane == 0, tile(ref, plane, r, j + 1), x), LANE - 1, 1)

    def over(body, r0, rstep, nr, j0=0, jstep=1, nj=col_tiles, unroll=4):
        def step(i, carry):
            body(r0 + i // nj * rstep, j0 + i % nj * jstep)
            return carry

        lax.fori_loop(0, nr * nj, step, 0, unroll=unroll)

    def sums(r, j):
        parts_s, parts_w = [], []
        for k in range(classes):
            x = tile(field, k, r, j)
            parts_s.append(x)
            parts_w.append(speed[k] * x)
        while len(parts_s) > 1:
            parts_s = [a + b for a, b in zip(parts_s[::2], parts_s[1::2])]
            parts_w = [a + b for a, b in zip(parts_w[::2], parts_w[1::2])]
        partial[(0, *at(r, j))] = parts_s[0]
        partial[(1, *at(r, j))] = parts_w[0]

    for r in range(row_tiles):
        loads[r].wait()
        over(sums, r, 1, 1, unroll=2)

    for copy in statics:
        copy.wait()

    def statics_of(r, j):
        kind = mask_v[at(r, j)]
        put(field, classes + WETTED, r, j, (kind > 0).astype(jnp.float32))
        put(field, classes + BED, r, j, jnp.where(kind == 2, TIME_STEP, 0.0) / depth_v[at(r, j)])

    over(statics_of, 0, 1, row_tiles)

    def pack_cols(ref, count, dst, slot, tile_rows):
        for i, r in enumerate(tile_rows):
            head = jnp.zeros((SUB, LANE), jnp.float32)
            tail = jnp.zeros((SUB, LANE), jnp.float32)
            for p in range(count):
                x = tile(ref, p, r, 0)
                head = jnp.where(lane == p, pltpu.roll(x, p, 1) if p else x, head)
                x = tile(ref, p, r, col_tiles - 1)
                tail = jnp.where(lane == p, pltpu.roll(x, p + 1, 1), tail)
            dst[(slot, *at(i, 0))] = head
            dst[(slot + 1, *at(i, 0))] = tail

    own_tiles = tuple(range(row_tiles))
    outer_tiles = (-1, row_tiles)
    walls = (classes + WETTED,)

    pack_cols(field, classes + 3, pack, 0, own_tiles)

    used = []

    def send(src, dst, peer):
        index = len(used)
        used.append(index)
        copy = pltpu.make_async_remote_copy(
            src_ref=src,
            dst_ref=dst,
            send_sem=send_sem.at[index],
            recv_sem=recv_sem.at[index],
            device_id=peer,
            device_id_type=MESH,
        )
        copy.start()
        return copy

    pl.semaphore_wait(barrier, len(peers))

    shares = [send(partial.at[0], sibling.at[0], me_sibling)]

    def send_rows(start, count):
        some = pl.ds(start, count)
        return [
            send(
                field.at[some, pl.ds(SUB + rows - 2, 2), inner_cols],
                field.at[some, pl.ds(SUB - 2, 2), inner_cols],
                me_next,
            ),
            send(
                field.at[some, pl.ds(SUB, 2), inner_cols],
                field.at[some, pl.ds(SUB + rows, 2), inner_cols],
                me_prev,
            ),
        ]

    def send_cols(src, slot):
        return [
            send(src.at[slot], src.at[slot + 2], me_left),
            send(src.at[slot + 1], src.at[slot + 3], me_right),
        ]

    shares.append(send(partial.at[1], sibling.at[1], me_sibling))
    col_halo = send_cols(pack, 0)
    row_halo = send_rows(0, planes)
    head_tile, tail_tile = pl.ds(0, SUB), pl.ds(rows - SUB, SUB)
    upper, lower = pl.ds(0, SUB), pl.ds(SUB, SUB)
    corners = [
        send(pack.at[1, tail_tile], corner.at[1, upper], next_right),
        send(pack.at[1, head_tile], corner.at[1, lower], prev_right),
        send(pack.at[0, tail_tile], corner.at[0, upper], next_left),
        send(pack.at[0, head_tile], corner.at[0, lower], prev_left),
    ]

    def own_rows(t):
        return pl.ds(pl.multiple_of(SUB * (t + core * (last - 2 * t)), SUB), SUB)

    def other_rows(t):
        return pl.ds(pl.multiple_of(SUB * (t + (1 - core) * (last - 2 * t)), SUB), SUB)

    far = []

    def chip_sums(q):
        shares[q].wait()
        for t in range(steps):
            own = own_rows(t)
            total[q, own, :] = partial[q, own, :] + sibling[q, own, :]
            far.append(send(total.at[q, own, :], remote.at[q, own, :], me_partner))
        for t in range(steps):
            other = other_rows(t)
            total[q, other, :] = partial[q, other, :] + sibling[q, other, :]

    chip_sums(0)
    edge_sums = []
    for source, after, before in ((0, me_next, me_prev), (1, far_next, far_prev)):
        edge_sums.append(
            send(total.at[0, pl.ds(rows - 1, 1), :], edges.at[source, 0, pl.ds(SUB - 1, 1), :], after)
        )
        edge_sums.append(send(total.at[0, pl.ds(0, 1), :], edges.at[source, 1, pl.ds(0, 1), :], before))

    def unpack_cols(ref, count, src, slot, tile_rows, walls):
        for i, r in enumerate(tile_rows):
            head = src[(slot, *at(i, 0))]
            tail = src[(slot + 1, *at(i, 0))]
            for p in range(count):
                right = pltpu.roll(head, LANE - p, 1) if p else head
                left = pltpu.roll(tail, LANE - 1 - p, 1)
                if p in walls:
                    right = jnp.where(cross < n_cross - 1, right, 0.0)
                    left = jnp.where(cross > 0, left, 0.0)
                put(ref, p, r, col_tiles, right)
                put(ref, p, r, -1, left)

    chip_sums(1)

    def coefficients(r, j, side=0):
        u = tile(field, classes + ALONG, r, j)
        v = tile(field, classes + ACROSS, r, j)
        w = tile(field, classes + WETTED, r, j)

        def face(speed_a, speed_b, wet_b):
            face_speed = 0.5 * (speed_a + speed_b)
            opening = TIME_STEP * (w * wet_b)
            ahead = opening * (jnp.maximum(face_speed, 0.0) + DIFFUSION)
            back = opening * (DIFFUSION - jnp.minimum(face_speed, 0.0))
            return ahead, back

        wet = classes + WETTED
        speed_plane = classes + ALONG
        from_north, to_north = face(
            u, north(field, speed_plane, r, j, u, side), north(field, wet, r, j, w, side)
        )
        to_south, from_south = face(
            u, south(field, speed_plane, r, j, u, side), south(field, wet, r, j, w, side)
        )
        from_west, to_west = face(v, west(field, classes + ACROSS, r, j, v), west(field, wet, r, j, w))
        to_east, from_east = face(v, east(field, classes + ACROSS, r, j, v), east(field, wet, r, j, w))
        coef[(0, *at(r + 1, j))] = from_north
        coef[(1, *at(r + 1, j))] = from_south
        coef[(2, *at(r + 1, j))] = from_west
        coef[(3, *at(r + 1, j))] = from_east
        coef[(4, *at(r + 1, j))] = 1.0 - ((to_north + to_south) + (to_west + to_east))

    def transported(ref, plane, r, j, factors, side=0):
        x = tile(ref, plane, r, j)
        along_part = factors[0] * north(ref, plane, r, j, x, side) + factors[1] * south(ref, plane, r, j, x, side)
        across_part = factors[2] * west(ref, plane, r, j, x) + factors[3] * east(ref, plane, r, j, x)
        return factors[4] * x + (along_part + across_part)

    def carry_first(r, j, side=0):
        factors = [coef[(i, *at(r + 1, j))] for i in range(5)]
        for k in range(classes):
            put(first, k, r, j, transported(field, k, r, j, factors, side))

    def both_first(r, j):
        coefficients(r, j)
        carry_first(r, j)

    over(both_first, 1, 1, row_tiles - 2, 1, 1, col_tiles - 2)
    for copy in col_halo:
        copy.wait_recv()
    unpack_cols(field, classes + 3, pack, 2, own_tiles, walls)
    over(both_first, 1, 1, row_tiles - 2, 0, col_tiles - 1, 2)

    def section_one(r, j, solids, keep_gain):
        put(first, classes, r, j, solids)
        g = tile(field, classes + BED, r, j) * hindered(solids)
        if keep_gain:
            gain[at(r, j)] = g
        for k in range(classes):
            put(first, k, r, j, tile(first, k, r, j) - (speed[k] * g) * tile(field, k, r, j))

    forwards = []

    def forward(q):
        sent = []
        for t in range(steps):
            far[q * steps + t].wait_recv()
            own = own_rows(t)
            sent.append((send(remote.at[q, own, :], remote.at[q, own, :], me_sibling), used[-1], t))
        forwards.extend(copy for copy, _, _ in sent)
        return sent

    def arrived(q, sent):
        for _, index, t in sent:
            other = other_rows(t)
            pltpu.make_async_remote_copy(
                src_ref=remote.at[q, other, :],
                dst_ref=remote.at[q, other, :],
                send_sem=send_sem.at[index],
                recv_sem=recv_sem.at[index],
                device_id=me_sibling,
                device_id_type=MESH,
            ).wait_recv()

    solids_sent = forward(0)
    for copy in row_halo:
        copy.wait_recv()
    over(both_first, 0, last, 2)
    arrived(0, solids_sent)

    def section_one_own(r, j):
        section_one(r, j, total[(0, *at(r, j))] + remote[(0, *at(r, j))], True)

    over(section_one_own, 0, 1, row_tiles)
    pack_cols(first, classes + 1, pack, 4, own_tiles)
    col_halo_one = send_cols(pack, 4)

    for copy in edge_sums + corners:
        copy.wait_recv()
    unpack_cols(field, classes + 3, corner, 0, outer_tiles, walls)
    for side, r in ((-1, -1), (1, row_tiles)):

        def outer(_, j, side=side, r=r):
            coefficients(r, j, side)
            carry_first(r, j, side)
            low = 0 if side < 0 else 1
            strip = pl.ds(pl.multiple_of(j * LANE, LANE), LANE)
            section_one(r, j, edges[0, low, :, strip] + edges[1, low, :, strip], False)

        over(outer, r, 1, 1, unroll=2)

    def carry_second(r, j):
        factors = [coef[(i, *at(r + 1, j))] for i in range(5)]
        for k in range(classes):
            value = tile(field, k, r, j) + transported(first, k, r, j, factors)
            out[(k, *at(r, j))] = 0.5 * value
        moved[at(r, j)] = transported(first, classes, r, j, factors)

    over(carry_second, 0, 1, row_tiles, 1, 1, col_tiles - 2)
    weighted_sent = forward(1)
    for copy in col_halo_one:
        copy.wait_recv()
    unpack_cols(first, classes + 1, pack, 6, own_tiles, ())
    over(carry_second, 0, 1, row_tiles, 0, col_tiles - 1, 2)
    arrived(1, weighted_sent)

    def finish(r, j):
        weighted = total[(1, *at(r, j))] + remote[(1, *at(r, j))]
        solids = moved[at(r, j)] - gain[at(r, j)] * weighted
        g = (0.5 * tile(field, classes + BED, r, j)) * hindered(solids)
        for k in range(classes):
            out[(k, *at(r, j))] = out[(k, *at(r, j))] - (speed[k] * g) * tile(first, k, r, j)

    over(finish, 0, 1, row_tiles)

    for copy in far + edge_sums + row_halo + col_halo + corners + forwards + col_halo_one:
        copy.wait_send()


def per_device(concentration, class_table, settle_speed, along_speed, across_speed, film_depth, cell_mask):
    classes, rows, cols = concentration.shape
    padded = (rows + 2 * SUB, cols + 2 * LANE)
    flat = (rows, cols)
    row_tiles = rows // SUB
    copies = 2 + 4 * (row_tiles // 2) + 14
    anywhere = pl.BlockSpec(memory_space=pl.ANY)
    f32 = jnp.float32

    def keep(array):
        return pltpu.with_memory_space_constraint(array, pltpu.HBM)

    return pl.pallas_call(
        section_kernel,
        out_shape=pltpu.VMEM(concentration.shape, f32),
        in_specs=[anywhere] * 7,
        out_specs=pl.BlockSpec(memory_space=pltpu.VMEM),
        scratch_shapes=[
            pltpu.SMEM(class_table.shape, jnp.int32),
            pltpu.SMEM(settle_speed.shape, f32),
            pltpu.VMEM((classes + 4, *padded), f32),
            pltpu.VMEM((classes + 1, *padded), f32),
            pltpu.VMEM((2, 2, SUB, cols), f32),
            pltpu.VMEM((2, *flat), f32),
            pltpu.VMEM((2, *flat), f32),
            pltpu.VMEM((2, *flat), f32),
            pltpu.VMEM((2, *flat), f32),
            pltpu.VMEM((5, rows + 2 * SUB, cols), f32),
            pltpu.VMEM(flat, f32),
            pltpu.VMEM(flat, f32),
            pltpu.VMEM(flat, f32),
            pltpu.VMEM(flat, jnp.int32),
            pltpu.VMEM((8, rows, LANE), f32),
            pltpu.VMEM((2, 2 * SUB, LANE), f32),
            pltpu.SemaphoreType.DMA((row_tiles + 6,)),
            pltpu.SemaphoreType.DMA((copies,)),
            pltpu.SemaphoreType.DMA((copies,)),
        ],
        compiler_params=pltpu.CompilerParams(
            collective_id=0, has_side_effects=True, vmem_limit_bytes=32 * 2**20
        ),
        cost_estimate=pl.CostEstimate(
            flops=40 * classes * rows * cols, bytes_accessed=8 * classes * rows * cols, transcendentals=4 * rows * cols
        ),
    )(*map(keep, (concentration, class_table, settle_speed, along_speed, across_speed, film_depth, cell_mask)))


def solution(mesh):
    grid = P("helix", "cross")
    return jax.shard_map(
        per_device,
        mesh=mesh,
        in_specs=(P("cls", "helix", "cross"), P("cls"), P(), grid, grid, grid, grid),
        out_specs=P("cls", "helix", "cross"),
        check_vma=False,
    )
```

```python
import jax
import jax.numpy as jnp
from jax import lax
from jax.experimental import pallas as pl
from jax.experimental.pallas import tpu as pltpu
from jax.sharding import PartitionSpec as P

TIME_STEP = 0.25
DIFFUSION = 0.1
VOLUME_PER_UNIT = 0.01
EXPONENT = 4.65

MESH = pl.DeviceIdType.MESH
SUB, LANE = 8, 128
ALONG, ACROSS, WETTED, BED = 0, 1, 2, 3


def hindered(solids):
    return jnp.exp(EXPONENT * jnp.log(1.0 - VOLUME_PER_UNIT * solids))


def section_kernel(
    conc,
    table,
    settle,
    along,
    across,
    depth,
    mask,
    out,
    table_s,
    settle_s,
    field,
    first,
    edges,
    total,
    partial,
    sibling,
    remote,
    coef,
    gain,
    moved,
    depth_v,
    mask_v,
    pack,
    corner,
    load_sem,
    send_sem,
    recv_sem,
    ready_sem,
):
    classes, rows, cols = conc.shape
    row_tiles, col_tiles = rows // SUB, cols // LANE
    helix, cross, cls = lax.axis_index("helix"), lax.axis_index("cross"), lax.axis_index("cls")
    n_helix, n_cross = lax.axis_size("helix"), lax.axis_size("cross")
    core, half = cls % 2, cls // 2
    me_sibling = (helix, cross, half * 2 + 1 - core)
    me_partner = (helix, cross, (1 - half) * 2 + core)
    me_prev = ((helix + n_helix - 1) % n_helix, cross, cls)
    me_next = ((helix + 1) % n_helix, cross, cls)
    far_prev = ((helix + n_helix - 1) % n_helix, cross, (1 - half) * 2 + core)
    far_next = ((helix + 1) % n_helix, cross, (1 - half) * 2 + core)
    me_left = (helix, (cross + n_cross - 1) % n_cross, cls)
    me_right = (helix, (cross + 1) % n_cross, cls)

    prev_left, prev_right = (me_prev[0], me_left[1], cls), (me_prev[0], me_right[1], cls)
    next_left, next_right = (me_next[0], me_left[1], cls), (me_next[0], me_right[1], cls)

    inner_cols = pl.ds(LANE, cols)
    last = row_tiles - 1
    steps = row_tiles // 2
    planes = classes + 4

    loads = [
        pltpu.make_async_copy(
            conc.at[:, pl.ds(r * SUB, SUB), :],
            field.at[pl.ds(0, classes), pl.ds(SUB + r * SUB, SUB), inner_cols],
            load_sem.at[r],
        )
        for r in range(row_tiles)
    ]
    scalars = [
        pltpu.make_async_copy(table, table_s, load_sem.at[row_tiles + 4]),
        pltpu.make_async_copy(settle, settle_s, load_sem.at[row_tiles + 5]),
    ]
    inner = pl.ds(SUB, rows)
    statics = [
        pltpu.make_async_copy(along, field.at[classes + ALONG, inner, inner_cols], load_sem.at[row_tiles]),
        pltpu.make_async_copy(across, field.at[classes + ACROSS, inner, inner_cols], load_sem.at[row_tiles + 1]),
        pltpu.make_async_copy(depth, depth_v, load_sem.at[row_tiles + 2]),
        pltpu.make_async_copy(mask, mask_v, load_sem.at[row_tiles + 3]),
    ]
    for copy in scalars + loads + statics:
        copy.start()

    barrier = pltpu.get_barrier_semaphore()
    rank = half * n_helix + helix
    near_peers = (me_sibling, me_left, me_right)
    far_peers = (
        me_partner, me_prev, me_next, far_prev, far_next, prev_left, prev_right, next_left, next_right
    )
    inverse = (0, 2, 1, 4, 3, 8, 7, 6, 5)
    PARTNER, PREV, NEXT, FAR_PREV, FAR_NEXT, PREV_LEFT, PREV_RIGHT, NEXT_LEFT, NEXT_RIGHT = range(9)
    ranks = [peer[2] // 2 * n_helix + peer[0] for peer in far_peers]
    higher = [other - rank > 1 for other in ranks]
    lower = [rank - other > 1 for other in ranks]
    expected = len(near_peers)
    for peer in near_peers:
        pl.semaphore_signal(barrier, inc=1, device_id=peer, device_id_type=MESH)
    for i, peer in enumerate(far_peers):
        expected = expected + jnp.where(higher[i], 0, 1)

        @pl.when(jnp.logical_not(lower[i]))
        def _(peer=peer):
            pl.semaphore_signal(barrier, inc=1, device_id=peer, device_id_type=MESH)

    for copy in scalars:
        copy.wait()
    speed = [settle_s[table_s[k]] for k in range(classes)]
    sub = lax.broadcasted_iota(jnp.int32, (SUB, LANE), 0)
    lane = lax.broadcasted_iota(jnp.int32, (SUB, LANE), 1)

    def at(r, j):
        return pl.ds(pl.multiple_of(r * SUB, SUB), SUB), pl.ds(pl.multiple_of(j * LANE, LANE), LANE)

    def tile(ref, plane, r, j):
        return ref[(plane, *at(r + 1, j + 1))]

    def put(ref, plane, r, j, value):
        ref[(plane, *at(r + 1, j + 1))] = value

    def north(ref, plane, r, j, x, side=0):
        if side >= 0:
            x = jnp.where(sub == SUB - 1, tile(ref, plane, r - 1, j), x)
        return pltpu.roll(x, 1, 0)

    def south(ref, plane, r, j, x, side=0):
        if side <= 0:
            x = jnp.where(sub == 0, tile(ref, plane, r + 1, j), x)
        return pltpu.roll(x, SUB - 1, 0)

    def west(ref, plane, r, j, x):
        return pltpu.roll(jnp.where(lane == LANE - 1, tile(ref, plane, r, j - 1), x), 1, 1)

    def east(ref, plane, r, j, x):
        return pltpu.roll(jnp.where(lane == 0, tile(ref, plane, r, j + 1), x), LANE - 1, 1)

    def over(body, r0, rstep, nr, j0=0, jstep=1, nj=col_tiles, unroll=4):
        def step(i, carry):
            body(r0 + i // nj * rstep, j0 + i % nj * jstep)
            return carry

        lax.fori_loop(0, nr * nj, step, 0, unroll=unroll)

    def sums(r, j):
        parts_s, parts_w = [], []
        for k in range(classes):
            x = tile(field, k, r, j)
            parts_s.append(x)
            parts_w.append(speed[k] * x)
        while len(parts_s) > 1:
            parts_s = [a + b for a, b in zip(parts_s[::2], parts_s[1::2])]
            parts_w = [a + b for a, b in zip(parts_w[::2], parts_w[1::2])]
        partial[(0, *at(r, j))] = parts_s[0]
        partial[(1, *at(r, j))] = parts_w[0]

    for r in range(row_tiles):
        loads[r].wait()
        over(sums, r, 1, 1, unroll=2)

    for copy in statics:
        copy.wait()

    def statics_of(r, j):
        kind = mask_v[at(r, j)]
        put(field, classes + WETTED, r, j, (kind > 0).astype(jnp.float32))
        put(field, classes + BED, r, j, jnp.where(kind == 2, TIME_STEP, 0.0) / depth_v[at(r, j)])

    over(statics_of, 0, 1, row_tiles)

    def pack_cols(ref, count, dst, slot, tile_rows):
        for i, r in enumerate(tile_rows):
            head = jnp.zeros((SUB, LANE), jnp.float32)
            tail = jnp.zeros((SUB, LANE), jnp.float32)
            for p in range(count):
                x = tile(ref, p, r, 0)
                head = jnp.where(lane == p, pltpu.roll(x, p, 1) if p else x, head)
                x = tile(ref, p, r, col_tiles - 1)
                tail = jnp.where(lane == p, pltpu.roll(x, p + 1, 1), tail)
            dst[(slot, *at(i, 0))] = head
            dst[(slot + 1, *at(i, 0))] = tail

    own_tiles = tuple(range(row_tiles))
    outer_tiles = (-1, row_tiles)
    walls = (classes + WETTED,)

    pack_cols(field, classes + 3, pack, 0, own_tiles)

    used = []

    held = [[] for _ in far_peers]

    def send(src, dst, peer, relation=None):
        peer = peer if relation is None else far_peers[relation]
        index = len(used)
        used.append(index)
        copy = pltpu.make_async_remote_copy(
            src_ref=src,
            dst_ref=dst,
            send_sem=send_sem.at[index],
            recv_sem=recv_sem.at[index],
            device_id=peer,
            device_id_type=MESH,
        )
        if relation is None:
            copy.start()
        else:
            pl.when(jnp.logical_not(higher[relation]))(copy.start)
            held[relation].append(copy)
        return copy

    def release():
        for i, copies in enumerate(held):

            @pl.when(higher[i])
            def _(i=i, copies=copies):
                pl.semaphore_wait(ready_sem.at[i], 1)
                for copy in copies:
                    copy.start()

    pl.semaphore_wait(barrier, expected)
    for i, peer in enumerate(far_peers):

        @pl.when(lower[i])
        def _(i=i, peer=peer):
            pl.semaphore_signal(ready_sem.at[inverse[i]], inc=1, device_id=peer, device_id_type=MESH)

    shares = [send(partial.at[0], sibling.at[0], me_sibling)]

    def send_rows(start, count):
        some = pl.ds(start, count)
        return [
            send(
                field.at[some, pl.ds(SUB + rows - 2, 2), inner_cols],
                field.at[some, pl.ds(SUB - 2, 2), inner_cols],
                None,
                NEXT,
            ),
            send(
                field.at[some, pl.ds(SUB, 2), inner_cols],
                field.at[some, pl.ds(SUB + rows, 2), inner_cols],
                None,
                PREV,
            ),
        ]

    def send_cols(src, slot):
        return [
            send(src.at[slot], src.at[slot + 2], me_left),
            send(src.at[slot + 1], src.at[slot + 3], me_right),
        ]

    shares.append(send(partial.at[1], sibling.at[1], me_sibling))
    col_halo = send_cols(pack, 0)
    row_halo = send_rows(0, planes)
    head_tile, tail_tile = pl.ds(0, SUB), pl.ds(rows - SUB, SUB)
    upper, lower = pl.ds(0, SUB), pl.ds(SUB, SUB)
    corners = [
        send(pack.at[1, tail_tile], corner.at[1, upper], None, NEXT_RIGHT),
        send(pack.at[1, head_tile], corner.at[1, lower], None, PREV_RIGHT),
        send(pack.at[0, tail_tile], corner.at[0, upper], None, NEXT_LEFT),
        send(pack.at[0, head_tile], corner.at[0, lower], None, PREV_LEFT),
    ]

    def own_rows(t):
        return pl.ds(pl.multiple_of(SUB * (t + core * (last - 2 * t)), SUB), SUB)

    def other_rows(t):
        return pl.ds(pl.multiple_of(SUB * (t + (1 - core) * (last - 2 * t)), SUB), SUB)

    far = []

    def chip_sums(q):
        shares[q].wait()
        for t in range(steps):
            own = own_rows(t)
            total[q, own, :] = partial[q, own, :] + sibling[q, own, :]
            far.append(send(total.at[q, own, :], remote.at[q, own, :], None, PARTNER))
        for t in range(steps):
            other = other_rows(t)
            total[q, other, :] = partial[q, other, :] + sibling[q, other, :]

    chip_sums(0)
    edge_sums = []
    for source, after, before in ((0, NEXT, PREV), (1, FAR_NEXT, FAR_PREV)):
        edge_sums.append(
            send(total.at[0, pl.ds(rows - 1, 1), :], edges.at[source, 0, pl.ds(SUB - 1, 1), :], None, after)
        )
        edge_sums.append(send(total.at[0, pl.ds(0, 1), :], edges.at[source, 1, pl.ds(0, 1), :], None, before))

    def unpack_cols(ref, count, src, slot, tile_rows, walls):
        for i, r in enumerate(tile_rows):
            head = src[(slot, *at(i, 0))]
            tail = src[(slot + 1, *at(i, 0))]
            for p in range(count):
                right = pltpu.roll(head, LANE - p, 1) if p else head
                left = pltpu.roll(tail, LANE - 1 - p, 1)
                if p in walls:
                    right = jnp.where(cross < n_cross - 1, right, 0.0)
                    left = jnp.where(cross > 0, left, 0.0)
                put(ref, p, r, col_tiles, right)
                put(ref, p, r, -1, left)

    chip_sums(1)

    def coefficients(r, j, side=0):
        u = tile(field, classes + ALONG, r, j)
        v = tile(field, classes + ACROSS, r, j)
        w = tile(field, classes + WETTED, r, j)

        def face(speed_a, speed_b, wet_b):
            face_speed = 0.5 * (speed_a + speed_b)
            opening = TIME_STEP * (w * wet_b)
            ahead = opening * (jnp.maximum(face_speed, 0.0) + DIFFUSION)
            back = opening * (DIFFUSION - jnp.minimum(face_speed, 0.0))
            return ahead, back

        wet = classes + WETTED
        speed_plane = classes + ALONG
        from_north, to_north = face(
            u, north(field, speed_plane, r, j, u, side), north(field, wet, r, j, w, side)
        )
        to_south, from_south = face(
            u, south(field, speed_plane, r, j, u, side), south(field, wet, r, j, w, side)
        )
        from_west, to_west = face(v, west(field, classes + ACROSS, r, j, v), west(field, wet, r, j, w))
        to_east, from_east = face(v, east(field, classes + ACROSS, r, j, v), east(field, wet, r, j, w))
        coef[(0, *at(r + 1, j))] = from_north
        coef[(1, *at(r + 1, j))] = from_south
        coef[(2, *at(r + 1, j))] = from_west
        coef[(3, *at(r + 1, j))] = from_east
        coef[(4, *at(r + 1, j))] = 1.0 - ((to_north + to_south) + (to_west + to_east))

    def transported(ref, plane, r, j, factors, side=0):
        x = tile(ref, plane, r, j)
        along_part = factors[0] * north(ref, plane, r, j, x, side) + factors[1] * south(ref, plane, r, j, x, side)
        across_part = factors[2] * west(ref, plane, r, j, x) + factors[3] * east(ref, plane, r, j, x)
        return factors[4] * x + (along_part + across_part)

    def carry_first(r, j, side=0):
        factors = [coef[(i, *at(r + 1, j))] for i in range(5)]
        for k in range(classes):
            put(first, k, r, j, transported(field, k, r, j, factors, side))

    def both_first(r, j):
        coefficients(r, j)
        carry_first(r, j)

    over(both_first, 1, 1, row_tiles - 2, 1, 1, col_tiles - 2)
    for copy in col_halo:
        copy.wait_recv()
    unpack_cols(field, classes + 3, pack, 2, own_tiles, walls)
    over(both_first, 1, 1, row_tiles - 2, 0, col_tiles - 1, 2)

    def section_one(r, j, solids, keep_gain):
        put(first, classes, r, j, solids)
        g = tile(field, classes + BED, r, j) * hindered(solids)
        if keep_gain:
            gain[at(r, j)] = g
        for k in range(classes):
            put(first, k, r, j, tile(first, k, r, j) - (speed[k] * g) * tile(field, k, r, j))

    forwards = []

    def forward(q):
        sent = []
        for t in range(steps):
            far[q * steps + t].wait_recv()
            own = own_rows(t)
            sent.append((send(remote.at[q, own, :], remote.at[q, own, :], me_sibling), used[-1], t))
        forwards.extend(copy for copy, _, _ in sent)
        return sent

    def arrived(q, sent):
        for _, index, t in sent:
            other = other_rows(t)
            pltpu.make_async_remote_copy(
                src_ref=remote.at[q, other, :],
                dst_ref=remote.at[q, other, :],
                send_sem=send_sem.at[index],
                recv_sem=recv_sem.at[index],
                device_id=me_sibling,
                device_id_type=MESH,
            ).wait_recv()

    release()
    for copy in row_halo:
        copy.wait_recv()
    over(both_first, 0, last, 2)
    solids_sent = forward(0)
    arrived(0, solids_sent)

    def section_one_own(r, j):
        section_one(r, j, total[(0, *at(r, j))] + remote[(0, *at(r, j))], True)

    over(section_one_own, 0, 1, row_tiles)
    pack_cols(first, classes + 1, pack, 4, own_tiles)
    col_halo_one = send_cols(pack, 4)

    for copy in edge_sums + corners:
        copy.wait_recv()
    unpack_cols(field, classes + 3, corner, 0, outer_tiles, walls)
    for side, r in ((-1, -1), (1, row_tiles)):

        def outer(_, j, side=side, r=r):
            coefficients(r, j, side)
            carry_first(r, j, side)
            low = 0 if side < 0 else 1
            strip = pl.ds(pl.multiple_of(j * LANE, LANE), LANE)
            section_one(r, j, edges[0, low, :, strip] + edges[1, low, :, strip], False)

        over(outer, r, 1, 1, unroll=2)

    def carry_second(r, j):
        factors = [coef[(i, *at(r + 1, j))] for i in range(5)]
        for k in range(classes):
            value = tile(field, k, r, j) + transported(first, k, r, j, factors)
            out[(k, *at(r, j))] = 0.5 * value
        moved[at(r, j)] = transported(first, classes, r, j, factors)

    over(carry_second, 0, 1, row_tiles, 1, 1, col_tiles - 2)
    weighted_sent = forward(1)
    for copy in col_halo_one:
        copy.wait_recv()
    unpack_cols(first, classes + 1, pack, 6, own_tiles, ())
    over(carry_second, 0, 1, row_tiles, 0, col_tiles - 1, 2)
    arrived(1, weighted_sent)

    def finish(r, j):
        weighted = total[(1, *at(r, j))] + remote[(1, *at(r, j))]
        solids = moved[at(r, j)] - gain[at(r, j)] * weighted
        g = (0.5 * tile(field, classes + BED, r, j)) * hindered(solids)
        for k in range(classes):
            out[(k, *at(r, j))] = out[(k, *at(r, j))] - (speed[k] * g) * tile(first, k, r, j)

    over(finish, 0, 1, row_tiles)

    for copy in far + edge_sums + row_halo + col_halo + corners + forwards + col_halo_one:
        copy.wait_send()


def per_device(concentration, class_table, settle_speed, along_speed, across_speed, film_depth, cell_mask):
    classes, rows, cols = concentration.shape
    padded = (rows + 2 * SUB, cols + 2 * LANE)
    flat = (rows, cols)
    row_tiles = rows // SUB
    copies = 2 + 4 * (row_tiles // 2) + 14
    anywhere = pl.BlockSpec(memory_space=pl.ANY)
    f32 = jnp.float32

    def keep(array):
        return pltpu.with_memory_space_constraint(array, pltpu.HBM)

    return pl.pallas_call(
        section_kernel,
        out_shape=pltpu.VMEM(concentration.shape, f32),
        in_specs=[anywhere] * 7,
        out_specs=pl.BlockSpec(memory_space=pltpu.VMEM),
        scratch_shapes=[
            pltpu.SMEM(class_table.shape, jnp.int32),
            pltpu.SMEM(settle_speed.shape, f32),
            pltpu.VMEM((classes + 4, *padded), f32),
            pltpu.VMEM((classes + 1, *padded), f32),
            pltpu.VMEM((2, 2, SUB, cols), f32),
            pltpu.VMEM((2, *flat), f32),
            pltpu.VMEM((2, *flat), f32),
            pltpu.VMEM((2, *flat), f32),
            pltpu.VMEM((2, *flat), f32),
            pltpu.VMEM((5, rows + 2 * SUB, cols), f32),
            pltpu.VMEM(flat, f32),
            pltpu.VMEM(flat, f32),
            pltpu.VMEM(flat, f32),
            pltpu.VMEM(flat, jnp.int32),
            pltpu.VMEM((8, rows, LANE), f32),
            pltpu.VMEM((2, 2 * SUB, LANE), f32),
            pltpu.SemaphoreType.DMA((row_tiles + 6,)),
            pltpu.SemaphoreType.DMA((copies,)),
            pltpu.SemaphoreType.DMA((copies,)),
            pltpu.SemaphoreType.REGULAR((9,)),
        ],
        compiler_params=pltpu.CompilerParams(
            collective_id=0, has_side_effects=True, vmem_limit_bytes=32 * 2**20
        ),
        cost_estimate=pl.CostEstimate(
            flops=40 * classes * rows * cols, bytes_accessed=8 * classes * rows * cols, transcendentals=4 * rows * cols
        ),
    )(*map(keep, (concentration, class_table, settle_speed, along_speed, across_speed, film_depth, cell_mask)))


def solution(mesh):
    grid = P("helix", "cross")
    return jax.shard_map(
        per_device,
        mesh=mesh,
        in_specs=(P("cls", "helix", "cross"), P("cls"), P(), grid, grid, grid, grid),
        out_specs=P("cls", "helix", "cross"),
        check_vma=False,
    )
```

```python
import jax
import jax.numpy as jnp
from jax import lax
from jax.experimental import pallas as pl
from jax.experimental.pallas import tpu as pltpu
from jax.sharding import PartitionSpec as P

TIME_STEP = 0.25
DIFFUSION = 0.1
VOLUME_PER_UNIT = 0.01
EXPONENT = 4.65

MESH = pl.DeviceIdType.MESH
SUB, LANE = 8, 128
ALONG, ACROSS, WETTED, BED = 0, 1, 2, 3


def hindered(solids):
    return jnp.exp(EXPONENT * jnp.log(1.0 - VOLUME_PER_UNIT * solids))


def section_kernel(
    conc,
    table,
    settle,
    along,
    across,
    depth,
    mask,
    out,
    table_s,
    settle_s,
    field,
    first,
    edges,
    total,
    partial,
    sibling,
    remote,
    coef,
    gain,
    moved,
    depth_v,
    mask_v,
    pack,
    corner,
    load_sem,
    send_sem,
    recv_sem,
    ready_sem,
):
    classes, rows, cols = conc.shape
    row_tiles, col_tiles = rows // SUB, cols // LANE
    helix, cross, cls = lax.axis_index("helix"), lax.axis_index("cross"), lax.axis_index("cls")
    n_helix, n_cross = lax.axis_size("helix"), lax.axis_size("cross")
    core, half = cls % 2, cls // 2
    me_sibling = (helix, cross, half * 2 + 1 - core)
    me_partner = (helix, cross, (1 - half) * 2 + core)
    me_prev = ((helix + n_helix - 1) % n_helix, cross, cls)
    me_next = ((helix + 1) % n_helix, cross, cls)
    far_prev = ((helix + n_helix - 1) % n_helix, cross, (1 - half) * 2 + core)
    far_next = ((helix + 1) % n_helix, cross, (1 - half) * 2 + core)
    me_left = (helix, (cross + n_cross - 1) % n_cross, cls)
    me_right = (helix, (cross + 1) % n_cross, cls)

    prev_left, prev_right = (me_prev[0], me_left[1], cls), (me_prev[0], me_right[1], cls)
    next_left, next_right = (me_next[0], me_left[1], cls), (me_next[0], me_right[1], cls)

    inner_cols = pl.ds(LANE, cols)
    last = row_tiles - 1
    steps = row_tiles // 2
    planes = classes + 4

    loads = [
        pltpu.make_async_copy(
            conc.at[:, pl.ds(r * SUB, SUB), :],
            field.at[pl.ds(0, classes), pl.ds(SUB + r * SUB, SUB), inner_cols],
            load_sem.at[r],
        )
        for r in range(row_tiles)
    ]
    scalars = [
        pltpu.make_async_copy(table, table_s, load_sem.at[row_tiles + 4]),
        pltpu.make_async_copy(settle, settle_s, load_sem.at[row_tiles + 5]),
    ]
    inner = pl.ds(SUB, rows)
    statics = [
        pltpu.make_async_copy(along, field.at[classes + ALONG, inner, inner_cols], load_sem.at[row_tiles]),
        pltpu.make_async_copy(across, field.at[classes + ACROSS, inner, inner_cols], load_sem.at[row_tiles + 1]),
        pltpu.make_async_copy(depth, depth_v, load_sem.at[row_tiles + 2]),
        pltpu.make_async_copy(mask, mask_v, load_sem.at[row_tiles + 3]),
    ]
    for copy in scalars + loads + statics:
        copy.start()

    barrier = pltpu.get_barrier_semaphore()
    rank = (half * n_helix + helix) * n_cross + cross
    near_peers = (me_sibling,)
    far_peers = (
        me_partner, me_prev, me_next, far_prev, far_next, prev_left, prev_right, next_left, next_right, me_left, me_right
    )
    inverse = (0, 2, 1, 4, 3, 8, 7, 6, 5, 10, 9)
    PARTNER, PREV, NEXT, FAR_PREV, FAR_NEXT, PREV_LEFT, PREV_RIGHT, NEXT_LEFT, NEXT_RIGHT, LEFT, RIGHT = range(11)
    ranks = [(peer[2] // 2 * n_helix + peer[0]) * n_cross + peer[1] for peer in far_peers]
    higher = [other > rank for other in ranks]
    lower = [other < rank for other in ranks]
    close = [jnp.abs(other - rank) <= 2 * n_cross for other in ranks]
    expected = len(near_peers)
    for peer in near_peers:
        pl.semaphore_signal(barrier, inc=1, device_id=peer, device_id_type=MESH)
    for i, peer in enumerate(far_peers):
        expected = expected + jnp.where(higher[i], 0, 1)

        @pl.when(jnp.logical_not(lower[i]))
        def _(peer=peer):
            pl.semaphore_signal(barrier, inc=1, device_id=peer, device_id_type=MESH)

    for copy in scalars:
        copy.wait()
    speed = [settle_s[table_s[k]] for k in range(classes)]
    sub = lax.broadcasted_iota(jnp.int32, (SUB, LANE), 0)
    lane = lax.broadcasted_iota(jnp.int32, (SUB, LANE), 1)

    def at(r, j):
        return pl.ds(pl.multiple_of(r * SUB, SUB), SUB), pl.ds(pl.multiple_of(j * LANE, LANE), LANE)

    def tile(ref, plane, r, j):
        return ref[(plane, *at(r + 1, j + 1))]

    def put(ref, plane, r, j, value):
        ref[(plane, *at(r + 1, j + 1))] = value

    def north(ref, plane, r, j, x, side=0):
        if side >= 0:
            x = jnp.where(sub == SUB - 1, tile(ref, plane, r - 1, j), x)
        return pltpu.roll(x, 1, 0)

    def south(ref, plane, r, j, x, side=0):
        if side <= 0:
            x = jnp.where(sub == 0, tile(ref, plane, r + 1, j), x)
        return pltpu.roll(x, SUB - 1, 0)

    def west(ref, plane, r, j, x):
        return pltpu.roll(jnp.where(lane == LANE - 1, tile(ref, plane, r, j - 1), x), 1, 1)

    def east(ref, plane, r, j, x):
        return pltpu.roll(jnp.where(lane == 0, tile(ref, plane, r, j + 1), x), LANE - 1, 1)

    def over(body, r0, rstep, nr, j0=0, jstep=1, nj=col_tiles, unroll=4):
        def step(i, carry):
            body(r0 + i // nj * rstep, j0 + i % nj * jstep)
            return carry

        lax.fori_loop(0, nr * nj, step, 0, unroll=unroll)

    def sums(r, j):
        parts_s, parts_w = [], []
        for k in range(classes):
            x = tile(field, k, r, j)
            parts_s.append(x)
            parts_w.append(speed[k] * x)
        while len(parts_s) > 1:
            parts_s = [a + b for a, b in zip(parts_s[::2], parts_s[1::2])]
            parts_w = [a + b for a, b in zip(parts_w[::2], parts_w[1::2])]
        partial[(0, *at(r, j))] = parts_s[0]
        partial[(1, *at(r, j))] = parts_w[0]

    for r in range(row_tiles):
        loads[r].wait()
        over(sums, r, 1, 1, unroll=2)

    def pack_cols(ref, count, dst, slot, tile_rows):
        for i, r in enumerate(tile_rows):
            head = jnp.zeros((SUB, LANE), jnp.float32)
            tail = jnp.zeros((SUB, LANE), jnp.float32)
            for p in range(count):
                x = tile(ref, p, r, 0)
                head = jnp.where(lane == p, pltpu.roll(x, p, 1) if p else x, head)
                x = tile(ref, p, r, col_tiles - 1)
                tail = jnp.where(lane == p, pltpu.roll(x, p + 1, 1), tail)
            dst[(slot, *at(i, 0))] = head
            dst[(slot + 1, *at(i, 0))] = tail

    own_tiles = tuple(range(row_tiles))
    outer_tiles = (-1, row_tiles)
    walls = (classes + WETTED,)

    used = []

    held = [[] for _ in far_peers]
    held_last = []
    calm = jnp.logical_and(half == 1, jnp.logical_and(8 * helix >= 2 * n_helix, 8 * helix < 4 * n_helix))
    patient = jnp.logical_and(half == 1, 8 * helix >= 5 * n_helix)

    def send(src, dst, peer, relation=None, later=False):
        peer = peer if relation is None else far_peers[relation]
        index = len(used)
        used.append(index)
        copy = pltpu.make_async_remote_copy(
            src_ref=src,
            dst_ref=dst,
            send_sem=send_sem.at[index],
            recv_sem=recv_sem.at[index],
            device_id=peer,
            device_id_type=MESH,
        )
        if relation is None:
            copy.start()
        else:
            now = jnp.logical_not(higher[relation])
            if later:
                now = jnp.logical_and(now, jnp.logical_not(jnp.logical_or(patient, calm)))
            pl.when(now)(copy.start)
            (held_last if later else held[relation]).append(copy)
        return copy

    def release(near):
        for i, copies in enumerate(held):

            @pl.when(jnp.logical_and(higher[i], close[i] if near else jnp.logical_not(close[i])))
            def _(i=i, copies=copies):
                pl.semaphore_wait(ready_sem.at[i], 1)
                for copy in copies:
                    copy.start()

    pl.semaphore_wait(barrier, expected)
    for i, peer in enumerate(far_peers):

        @pl.when(lower[i])
        def _(i=i, peer=peer):
            pl.semaphore_signal(ready_sem.at[inverse[i]], inc=1, device_id=peer, device_id_type=MESH)

    shares = [send(partial.at[0], sibling.at[0], me_sibling)]

    def send_rows(start, count):
        some = pl.ds(start, count)
        return [
            send(
                field.at[some, pl.ds(SUB + rows - 2, 2), inner_cols],
                field.at[some, pl.ds(SUB - 2, 2), inner_cols],
                None,
                NEXT,
            ),
            send(
                field.at[some, pl.ds(SUB, 2), inner_cols],
                field.at[some, pl.ds(SUB + rows, 2), inner_cols],
                None,
                PREV,
            ),
        ]

    def send_cols(src, slot, left, right):
        return [
            send(src.at[slot], src.at[slot + 2], me_left, left),
            send(src.at[slot + 1], src.at[slot + 3], me_right, right),
        ]

    shares.append(send(partial.at[1], sibling.at[1], me_sibling))
    for copy in statics:
        copy.wait()

    def statics_of(r, j):
        kind = mask_v[at(r, j)]
        put(field, classes + WETTED, r, j, (kind > 0).astype(jnp.float32))
        put(field, classes + BED, r, j, jnp.where(kind == 2, TIME_STEP, 0.0) / depth_v[at(r, j)])

    over(statics_of, 0, 1, row_tiles)

    pack_cols(field, classes + 3, pack, 0, own_tiles)

    col_halo = send_cols(pack, 0, LEFT, RIGHT)
    row_halo = send_rows(0, planes)
    head_tile, tail_tile = pl.ds(0, SUB), pl.ds(rows - SUB, SUB)
    upper, lower = pl.ds(0, SUB), pl.ds(SUB, SUB)
    corners = [
        send(pack.at[1, tail_tile], corner.at[1, upper], None, NEXT_RIGHT),
        send(pack.at[1, head_tile], corner.at[1, lower], None, PREV_RIGHT),
        send(pack.at[0, tail_tile], corner.at[0, upper], None, NEXT_LEFT),
        send(pack.at[0, head_tile], corner.at[0, lower], None, PREV_LEFT),
    ]

    def own_rows(t):
        return pl.ds(pl.multiple_of(SUB * (t + core * (last - 2 * t)), SUB), SUB)

    def other_rows(t):
        return pl.ds(pl.multiple_of(SUB * (t + (1 - core) * (last - 2 * t)), SUB), SUB)

    far = []

    def chip_sums(q):
        shares[q].wait()
        for t in range(steps):
            own = own_rows(t)
            total[q, own, :] = partial[q, own, :] + sibling[q, own, :]
            far.append(send(total.at[q, own, :], remote.at[q, own, :], None, PARTNER, q == 1))
        for t in range(steps):
            other = other_rows(t)
            total[q, other, :] = partial[q, other, :] + sibling[q, other, :]

    chip_sums(0)
    edge_sums = []
    for source, after, before in ((0, NEXT, PREV), (1, FAR_NEXT, FAR_PREV)):
        edge_sums.append(
            send(total.at[0, pl.ds(rows - 1, 1), :], edges.at[source, 0, pl.ds(SUB - 1, 1), :], None, after)
        )
        edge_sums.append(send(total.at[0, pl.ds(0, 1), :], edges.at[source, 1, pl.ds(0, 1), :], None, before))

    def unpack_cols(ref, count, src, slot, tile_rows, walls):
        for i, r in enumerate(tile_rows):
            head = src[(slot, *at(i, 0))]
            tail = src[(slot + 1, *at(i, 0))]
            for p in range(count):
                right = pltpu.roll(head, LANE - p, 1) if p else head
                left = pltpu.roll(tail, LANE - 1 - p, 1)
                if p in walls:
                    right = jnp.where(cross < n_cross - 1, right, 0.0)
                    left = jnp.where(cross > 0, left, 0.0)
                put(ref, p, r, col_tiles, right)
                put(ref, p, r, -1, left)

    chip_sums(1)

    def coefficients(r, j, side=0):
        u = tile(field, classes + ALONG, r, j)
        v = tile(field, classes + ACROSS, r, j)
        w = tile(field, classes + WETTED, r, j)

        def face(speed_a, speed_b, wet_b):
            face_speed = 0.5 * (speed_a + speed_b)
            opening = TIME_STEP * (w * wet_b)
            ahead = opening * (jnp.maximum(face_speed, 0.0) + DIFFUSION)
            back = opening * (DIFFUSION - jnp.minimum(face_speed, 0.0))
            return ahead, back

        wet = classes + WETTED
        speed_plane = classes + ALONG
        from_north, to_north = face(
            u, north(field, speed_plane, r, j, u, side), north(field, wet, r, j, w, side)
        )
        to_south, from_south = face(
            u, south(field, speed_plane, r, j, u, side), south(field, wet, r, j, w, side)
        )
        from_west, to_west = face(v, west(field, classes + ACROSS, r, j, v), west(field, wet, r, j, w))
        to_east, from_east = face(v, east(field, classes + ACROSS, r, j, v), east(field, wet, r, j, w))
        coef[(0, *at(r + 1, j))] = from_north
        coef[(1, *at(r + 1, j))] = from_south
        coef[(2, *at(r + 1, j))] = from_west
        coef[(3, *at(r + 1, j))] = from_east
        coef[(4, *at(r + 1, j))] = 1.0 - ((to_north + to_south) + (to_west + to_east))

    def transported(ref, plane, r, j, factors, side=0):
        x = tile(ref, plane, r, j)
        along_part = factors[0] * north(ref, plane, r, j, x, side) + factors[1] * south(ref, plane, r, j, x, side)
        across_part = factors[2] * west(ref, plane, r, j, x) + factors[3] * east(ref, plane, r, j, x)
        return factors[4] * x + (along_part + across_part)

    def carry_first(r, j, side=0):
        factors = [coef[(i, *at(r + 1, j))] for i in range(5)]
        for k in range(classes):
            put(first, k, r, j, transported(field, k, r, j, factors, side))

    def both_first(r, j):
        coefficients(r, j)
        carry_first(r, j)

    over(both_first, 1, 1, row_tiles - 2, 1, 1, col_tiles - 2)
    release(True)
    for copy in col_halo:
        copy.wait_recv()
    unpack_cols(field, classes + 3, pack, 2, own_tiles, walls)
    over(both_first, 1, 1, row_tiles - 2, 0, col_tiles - 1, 2)

    def section_one(r, j, solids, keep_gain):
        put(first, classes, r, j, solids)
        g = tile(field, classes + BED, r, j) * hindered(solids)
        if keep_gain:
            gain[at(r, j)] = g
        for k in range(classes):
            put(first, k, r, j, tile(first, k, r, j) - (speed[k] * g) * tile(field, k, r, j))

    forwards = []

    def forward(q):
        sent = []
        for t in range(steps):
            far[q * steps + t].wait_recv()
            own = own_rows(t)
            sent.append((send(remote.at[q, own, :], remote.at[q, own, :], me_sibling), used[-1], t))
        forwards.extend(copy for copy, _, _ in sent)
        return sent

    def arrived(q, sent):
        for _, index, t in sent:
            other = other_rows(t)
            pltpu.make_async_remote_copy(
                src_ref=remote.at[q, other, :],
                dst_ref=remote.at[q, other, :],
                send_sem=send_sem.at[index],
                recv_sem=recv_sem.at[index],
                device_id=me_sibling,
                device_id_type=MESH,
            ).wait_recv()

    release(False)
    for copy in row_halo:
        copy.wait_recv()
    over(both_first, 0, last, 2)

    @pl.when(calm)
    def _():
        for copy in held_last:
            copy.start()

    solids_sent = forward(0)

    @pl.when(jnp.logical_or(higher[PARTNER], patient))
    def _():
        for copy in held_last:
            copy.start()

    arrived(0, solids_sent)

    def section_one_own(r, j):
        section_one(r, j, total[(0, *at(r, j))] + remote[(0, *at(r, j))], True)

    over(section_one_own, 0, 1, row_tiles)
    pack_cols(first, classes + 1, pack, 4, own_tiles)
    col_halo_one = send_cols(pack, 4, None, None)

    for copy in edge_sums + corners:
        copy.wait_recv()
    unpack_cols(field, classes + 3, corner, 0, outer_tiles, walls)
    for side, r in ((-1, -1), (1, row_tiles)):

        def outer(_, j, side=side, r=r):
            coefficients(r, j, side)
            carry_first(r, j, side)
            low = 0 if side < 0 else 1
            strip = pl.ds(pl.multiple_of(j * LANE, LANE), LANE)
            section_one(r, j, edges[0, low, :, strip] + edges[1, low, :, strip], False)

        over(outer, r, 1, 1, unroll=2)

    def carry_second(r, j):
        factors = [coef[(i, *at(r + 1, j))] for i in range(5)]
        for k in range(classes):
            value = tile(field, k, r, j) + transported(first, k, r, j, factors)
            out[(k, *at(r, j))] = 0.5 * value
        moved[at(r, j)] = transported(first, classes, r, j, factors)

    over(carry_second, 0, 1, row_tiles, 1, 1, col_tiles - 2)
    weighted_sent = forward(1)
    for copy in col_halo_one:
        copy.wait_recv()
    unpack_cols(first, classes + 1, pack, 6, own_tiles, ())
    over(carry_second, 0, 1, row_tiles, 0, col_tiles - 1, 2)
    arrived(1, weighted_sent)

    def finish(r, j):
        weighted = total[(1, *at(r, j))] + remote[(1, *at(r, j))]
        solids = moved[at(r, j)] - gain[at(r, j)] * weighted
        g = (0.5 * tile(field, classes + BED, r, j)) * hindered(solids)
        for k in range(classes):
            out[(k, *at(r, j))] = out[(k, *at(r, j))] - (speed[k] * g) * tile(first, k, r, j)

    over(finish, 0, 1, row_tiles)

    for copy in far + edge_sums + row_halo + col_halo + corners + forwards + col_halo_one:
        copy.wait_send()


def per_device(concentration, class_table, settle_speed, along_speed, across_speed, film_depth, cell_mask):
    classes, rows, cols = concentration.shape
    padded = (rows + 2 * SUB, cols + 2 * LANE)
    flat = (rows, cols)
    row_tiles = rows // SUB
    copies = 2 + 4 * (row_tiles // 2) + 14
    anywhere = pl.BlockSpec(memory_space=pl.ANY)
    f32 = jnp.float32

    def keep(array):
        return pltpu.with_memory_space_constraint(array, pltpu.HBM)

    return pl.pallas_call(
        section_kernel,
        out_shape=pltpu.VMEM(concentration.shape, f32),
        in_specs=[anywhere] * 7,
        out_specs=pl.BlockSpec(memory_space=pltpu.VMEM),
        scratch_shapes=[
            pltpu.SMEM(class_table.shape, jnp.int32),
            pltpu.SMEM(settle_speed.shape, f32),
            pltpu.VMEM((classes + 4, *padded), f32),
            pltpu.VMEM((classes + 1, *padded), f32),
            pltpu.VMEM((2, 2, SUB, cols), f32),
            pltpu.VMEM((2, *flat), f32),
            pltpu.VMEM((2, *flat), f32),
            pltpu.VMEM((2, *flat), f32),
            pltpu.VMEM((2, *flat), f32),
            pltpu.VMEM((5, rows + 2 * SUB, cols), f32),
            pltpu.VMEM(flat, f32),
            pltpu.VMEM(flat, f32),
            pltpu.VMEM(flat, f32),
            pltpu.VMEM(flat, jnp.int32),
            pltpu.VMEM((8, rows, LANE), f32),
            pltpu.VMEM((2, 2 * SUB, LANE), f32),
            pltpu.SemaphoreType.DMA((row_tiles + 6,)),
            pltpu.SemaphoreType.DMA((copies,)),
            pltpu.SemaphoreType.DMA((copies,)),
            pltpu.SemaphoreType.REGULAR((11,)),
        ],
        compiler_params=pltpu.CompilerParams(
            collective_id=0, has_side_effects=True, vmem_limit_bytes=32 * 2**20
        ),
        cost_estimate=pl.CostEstimate(
            flops=40 * classes * rows * cols, bytes_accessed=8 * classes * rows * cols, transcendentals=4 * rows * cols
        ),
    )(*map(keep, (concentration, class_table, settle_speed, along_speed, across_speed, film_depth, cell_mask)))


def solution(mesh):
    grid = P("helix", "cross")
    return jax.shard_map(
        per_device,
        mesh=mesh,
        in_specs=(P("cls", "helix", "cross"), P("cls"), P(), grid, grid, grid, grid),
        out_specs=P("cls", "helix", "cross"),
        check_vma=False,
    )
```

```python
import jax
import jax.numpy as jnp
from jax import lax
from jax.experimental import pallas as pl
from jax.experimental.pallas import tpu as pltpu
from jax.sharding import PartitionSpec as P

TIME_STEP = 0.25
DIFFUSION = 0.1
VOLUME_PER_UNIT = 0.01
EXPONENT = 4.65

MESH = pl.DeviceIdType.MESH
SUB, LANE = 8, 128
ALONG, ACROSS, WETTED, BED = 0, 1, 2, 3


def hindered(solids):
    return jnp.exp(EXPONENT * jnp.log(1.0 - VOLUME_PER_UNIT * solids))


def section_kernel(
    conc,
    table,
    settle,
    along,
    across,
    depth,
    mask,
    out,
    table_s,
    settle_s,
    field,
    first,
    edges,
    total,
    partial,
    sibling,
    remote,
    coef,
    gain,
    moved,
    depth_v,
    mask_v,
    pack,
    corner,
    load_sem,
    send_sem,
    recv_sem,
    ready_sem,
):
    classes, rows, cols = conc.shape
    row_tiles, col_tiles = rows // SUB, cols // LANE
    helix, cross, cls = lax.axis_index("helix"), lax.axis_index("cross"), lax.axis_index("cls")
    n_helix, n_cross = lax.axis_size("helix"), lax.axis_size("cross")
    core, half = cls % 2, cls // 2
    me_sibling = (helix, cross, half * 2 + 1 - core)
    me_partner = (helix, cross, (1 - half) * 2 + core)
    me_prev = ((helix + n_helix - 1) % n_helix, cross, cls)
    me_next = ((helix + 1) % n_helix, cross, cls)
    far_prev = ((helix + n_helix - 1) % n_helix, cross, (1 - half) * 2 + core)
    far_next = ((helix + 1) % n_helix, cross, (1 - half) * 2 + core)
    me_left = (helix, (cross + n_cross - 1) % n_cross, cls)
    me_right = (helix, (cross + 1) % n_cross, cls)

    prev_left, prev_right = (me_prev[0], me_left[1], cls), (me_prev[0], me_right[1], cls)
    next_left, next_right = (me_next[0], me_left[1], cls), (me_next[0], me_right[1], cls)

    inner_cols = pl.ds(LANE, cols)
    last = row_tiles - 1
    steps = row_tiles // 2
    planes = classes + 4

    loads = [
        pltpu.make_async_copy(
            conc.at[:, pl.ds(r * SUB, SUB), :],
            field.at[pl.ds(0, classes), pl.ds(SUB + r * SUB, SUB), inner_cols],
            load_sem.at[r],
        )
        for r in range(row_tiles)
    ]
    scalars = [
        pltpu.make_async_copy(table, table_s, load_sem.at[row_tiles + 4]),
        pltpu.make_async_copy(settle, settle_s, load_sem.at[row_tiles + 5]),
    ]
    inner = pl.ds(SUB, rows)
    statics = [
        pltpu.make_async_copy(along, field.at[classes + ALONG, inner, inner_cols], load_sem.at[row_tiles]),
        pltpu.make_async_copy(across, field.at[classes + ACROSS, inner, inner_cols], load_sem.at[row_tiles + 1]),
        pltpu.make_async_copy(depth, depth_v, load_sem.at[row_tiles + 2]),
        pltpu.make_async_copy(mask, mask_v, load_sem.at[row_tiles + 3]),
    ]
    for copy in scalars + loads + statics:
        copy.start()

    barrier = pltpu.get_barrier_semaphore()
    rank = (half * n_helix + helix) * n_cross + cross
    near_peers = (me_sibling,)
    far_peers = (
        me_partner, me_prev, me_next, far_prev, far_next, prev_left, prev_right, next_left, next_right, me_left, me_right
    )
    inverse = (0, 2, 1, 4, 3, 8, 7, 6, 5, 10, 9)
    PARTNER, PREV, NEXT, FAR_PREV, FAR_NEXT, PREV_LEFT, PREV_RIGHT, NEXT_LEFT, NEXT_RIGHT, LEFT, RIGHT = range(11)
    ranks = [(peer[2] // 2 * n_helix + peer[0]) * n_cross + peer[1] for peer in far_peers]
    higher = [other > rank for other in ranks]
    lower = [other < rank for other in ranks]
    close = [jnp.abs(other - rank) <= 2 * n_cross for other in ranks]
    expected = len(near_peers)
    for peer in near_peers:
        pl.semaphore_signal(barrier, inc=1, device_id=peer, device_id_type=MESH)
    for i, peer in enumerate(far_peers):
        expected = expected + jnp.where(higher[i], 0, 1)

        @pl.when(jnp.logical_not(lower[i]))
        def _(peer=peer):
            pl.semaphore_signal(barrier, inc=1, device_id=peer, device_id_type=MESH)

    for copy in scalars:
        copy.wait()
    speed = [settle_s[table_s[k]] for k in range(classes)]
    sub = lax.broadcasted_iota(jnp.int32, (SUB, LANE), 0)
    lane = lax.broadcasted_iota(jnp.int32, (SUB, LANE), 1)

    def at(r, j):
        return pl.ds(pl.multiple_of(r * SUB, SUB), SUB), pl.ds(pl.multiple_of(j * LANE, LANE), LANE)

    def tile(ref, plane, r, j):
        return ref[(plane, *at(r + 1, j + 1))]

    def put(ref, plane, r, j, value):
        ref[(plane, *at(r + 1, j + 1))] = value

    def north(ref, plane, r, j, x, side=0):
        if side >= 0:
            x = jnp.where(sub == SUB - 1, tile(ref, plane, r - 1, j), x)
        return pltpu.roll(x, 1, 0)

    def south(ref, plane, r, j, x, side=0):
        if side <= 0:
            x = jnp.where(sub == 0, tile(ref, plane, r + 1, j), x)
        return pltpu.roll(x, SUB - 1, 0)

    def west(ref, plane, r, j, x):
        return pltpu.roll(jnp.where(lane == LANE - 1, tile(ref, plane, r, j - 1), x), 1, 1)

    def east(ref, plane, r, j, x):
        return pltpu.roll(jnp.where(lane == 0, tile(ref, plane, r, j + 1), x), LANE - 1, 1)

    def over(body, r0, rstep, nr, j0=0, jstep=1, nj=col_tiles, unroll=4):
        def step(i, carry):
            body(r0 + i // nj * rstep, j0 + i % nj * jstep)
            return carry

        lax.fori_loop(0, nr * nj, step, 0, unroll=unroll)

    def sums(r, j):
        parts_s, parts_w = [], []
        for k in range(classes):
            x = tile(field, k, r, j)
            parts_s.append(x)
            parts_w.append(speed[k] * x)
        while len(parts_s) > 1:
            parts_s = [a + b for a, b in zip(parts_s[::2], parts_s[1::2])]
            parts_w = [a + b for a, b in zip(parts_w[::2], parts_w[1::2])]
        partial[(0, *at(r, j))] = parts_s[0]
        partial[(1, *at(r, j))] = parts_w[0]

    for r in range(row_tiles):
        loads[r].wait()
        over(sums, r, 1, 1, unroll=4)

    def pack_cols(ref, count, dst, slot, tile_rows):
        for i, r in enumerate(tile_rows):
            head = jnp.zeros((SUB, LANE), jnp.float32)
            tail = jnp.zeros((SUB, LANE), jnp.float32)
            for p in range(count):
                x = tile(ref, p, r, 0)
                head = jnp.where(lane == p, pltpu.roll(x, p, 1) if p else x, head)
                x = tile(ref, p, r, col_tiles - 1)
                tail = jnp.where(lane == p, pltpu.roll(x, p + 1, 1), tail)
            dst[(slot, *at(i, 0))] = head
            dst[(slot + 1, *at(i, 0))] = tail

    own_tiles = tuple(range(row_tiles))
    outer_tiles = (-1, row_tiles)
    walls = (classes + WETTED,)

    used = []

    held = [[] for _ in far_peers]
    held_last = []
    calm = jnp.logical_and(half == 1, jnp.logical_and(8 * helix >= 2 * n_helix, 8 * helix < 4 * n_helix))
    patient = jnp.logical_and(half == 1, 8 * helix >= 5 * n_helix)

    def send(src, dst, peer, relation=None, later=False):
        peer = peer if relation is None else far_peers[relation]
        index = len(used)
        used.append(index)
        copy = pltpu.make_async_remote_copy(
            src_ref=src,
            dst_ref=dst,
            send_sem=send_sem.at[index],
            recv_sem=recv_sem.at[index],
            device_id=peer,
            device_id_type=MESH,
        )
        if relation is None:
            copy.start()
        else:
            now = jnp.logical_not(higher[relation])
            if later:
                now = jnp.logical_and(now, jnp.logical_not(jnp.logical_or(patient, calm)))
            pl.when(now)(copy.start)
            (held_last if later else held[relation]).append(copy)
        return copy

    def release(near):
        for i, copies in enumerate(held):

            @pl.when(jnp.logical_and(higher[i], close[i] if near else jnp.logical_not(close[i])))
            def _(i=i, copies=copies):
                pl.semaphore_wait(ready_sem.at[i], 1)
                for copy in copies:
                    copy.start()

    pl.semaphore_wait(barrier, expected)
    for i, peer in enumerate(far_peers):

        @pl.when(lower[i])
        def _(i=i, peer=peer):
            pl.semaphore_signal(ready_sem.at[inverse[i]], inc=1, device_id=peer, device_id_type=MESH)

    shares = [send(partial.at[0], sibling.at[0], me_sibling)]

    def send_rows(start, count):
        some = pl.ds(start, count)
        return [
            send(
                field.at[some, pl.ds(SUB + rows - 2, 2), inner_cols],
                field.at[some, pl.ds(SUB - 2, 2), inner_cols],
                None,
                NEXT,
            ),
            send(
                field.at[some, pl.ds(SUB, 2), inner_cols],
                field.at[some, pl.ds(SUB + rows, 2), inner_cols],
                None,
                PREV,
            ),
        ]

    def send_cols(src, slot, left, right):
        return [
            send(src.at[slot], src.at[slot + 2], me_left, left),
            send(src.at[slot + 1], src.at[slot + 3], me_right, right),
        ]

    shares.append(send(partial.at[1], sibling.at[1], me_sibling))
    for copy in statics:
        copy.wait()

    def statics_of(r, j):
        kind = mask_v[at(r, j)]
        put(field, classes + WETTED, r, j, (kind > 0).astype(jnp.float32))
        put(field, classes + BED, r, j, jnp.where(kind == 2, TIME_STEP, 0.0) / depth_v[at(r, j)])

    over(statics_of, 0, 1, row_tiles)

    pack_cols(field, classes + 3, pack, 0, own_tiles)

    col_halo = send_cols(pack, 0, LEFT, RIGHT)
    row_halo = send_rows(0, planes)
    head_tile, tail_tile = pl.ds(0, SUB), pl.ds(rows - SUB, SUB)
    upper, lower = pl.ds(0, SUB), pl.ds(SUB, SUB)
    corners = [
        send(pack.at[1, tail_tile], corner.at[1, upper], None, NEXT_RIGHT),
        send(pack.at[1, head_tile], corner.at[1, lower], None, PREV_RIGHT),
        send(pack.at[0, tail_tile], corner.at[0, upper], None, NEXT_LEFT),
        send(pack.at[0, head_tile], corner.at[0, lower], None, PREV_LEFT),
    ]

    def own_rows(t):
        return pl.ds(pl.multiple_of(SUB * (t + core * (last - 2 * t)), SUB), SUB)

    def other_rows(t):
        return pl.ds(pl.multiple_of(SUB * (t + (1 - core) * (last - 2 * t)), SUB), SUB)

    far = []

    def chip_sums(q):
        shares[q].wait()
        for t in range(steps):
            own = own_rows(t)
            total[q, own, :] = partial[q, own, :] + sibling[q, own, :]
            far.append(send(total.at[q, own, :], remote.at[q, own, :], None, PARTNER, q == 1))
        for t in range(steps):
            other = other_rows(t)
            total[q, other, :] = partial[q, other, :] + sibling[q, other, :]

    chip_sums(0)
    edge_sums = []
    for source, after, before in ((0, NEXT, PREV), (1, FAR_NEXT, FAR_PREV)):
        edge_sums.append(
            send(total.at[0, pl.ds(rows - 1, 1), :], edges.at[source, 0, pl.ds(SUB - 1, 1), :], None, after)
        )
        edge_sums.append(send(total.at[0, pl.ds(0, 1), :], edges.at[source, 1, pl.ds(0, 1), :], None, before))

    def unpack_cols(ref, count, src, slot, tile_rows, walls):
        for i, r in enumerate(tile_rows):
            head = src[(slot, *at(i, 0))]
            tail = src[(slot + 1, *at(i, 0))]
            for p in range(count):
                right = pltpu.roll(head, LANE - p, 1) if p else head
                left = pltpu.roll(tail, LANE - 1 - p, 1)
                if p in walls:
                    right = jnp.where(cross < n_cross - 1, right, 0.0)
                    left = jnp.where(cross > 0, left, 0.0)
                put(ref, p, r, col_tiles, right)
                put(ref, p, r, -1, left)

    chip_sums(1)

    def coefficients(r, j, side=0):
        u = tile(field, classes + ALONG, r, j)
        v = tile(field, classes + ACROSS, r, j)
        w = tile(field, classes + WETTED, r, j)

        def face(speed_a, speed_b, wet_b):
            face_speed = 0.5 * (speed_a + speed_b)
            opening = TIME_STEP * (w * wet_b)
            ahead = opening * (jnp.maximum(face_speed, 0.0) + DIFFUSION)
            back = opening * (DIFFUSION - jnp.minimum(face_speed, 0.0))
            return ahead, back

        wet = classes + WETTED
        speed_plane = classes + ALONG
        from_north, to_north = face(
            u, north(field, speed_plane, r, j, u, side), north(field, wet, r, j, w, side)
        )
        to_south, from_south = face(
            u, south(field, speed_plane, r, j, u, side), south(field, wet, r, j, w, side)
        )
        from_west, to_west = face(v, west(field, classes + ACROSS, r, j, v), west(field, wet, r, j, w))
        to_east, from_east = face(v, east(field, classes + ACROSS, r, j, v), east(field, wet, r, j, w))
        coef[(0, *at(r + 1, j))] = from_north
        coef[(1, *at(r + 1, j))] = from_south
        coef[(2, *at(r + 1, j))] = from_west
        coef[(3, *at(r + 1, j))] = from_east
        coef[(4, *at(r + 1, j))] = 1.0 - ((to_north + to_south) + (to_west + to_east))

    def transported(ref, plane, r, j, factors, side=0):
        x = tile(ref, plane, r, j)
        along_part = factors[0] * north(ref, plane, r, j, x, side) + factors[1] * south(ref, plane, r, j, x, side)
        across_part = factors[2] * west(ref, plane, r, j, x) + factors[3] * east(ref, plane, r, j, x)
        return factors[4] * x + (along_part + across_part)

    def carry_first(r, j, side=0):
        factors = [coef[(i, *at(r + 1, j))] for i in range(5)]
        for k in range(classes):
            put(first, k, r, j, transported(field, k, r, j, factors, side))

    def both_first(r, j):
        coefficients(r, j)
        carry_first(r, j)

    over(both_first, 1, 1, row_tiles - 2, 1, 1, col_tiles - 2)
    release(True)
    for copy in col_halo:
        copy.wait_recv()
    unpack_cols(field, classes + 3, pack, 2, own_tiles, walls)
    over(both_first, 1, 1, row_tiles - 2, 0, col_tiles - 1, 2)

    def section_one(r, j, solids, keep_gain):
        put(first, classes, r, j, solids)
        g = tile(field, classes + BED, r, j) * hindered(solids)
        if keep_gain:
            gain[at(r, j)] = g
        for k in range(classes):
            put(first, k, r, j, tile(first, k, r, j) - (speed[k] * g) * tile(field, k, r, j))

    forwards = []

    def forward(q):
        sent = []
        for t in range(steps):
            far[q * steps + t].wait_recv()
            own = own_rows(t)
            sent.append((send(remote.at[q, own, :], remote.at[q, own, :], me_sibling), used[-1], t))
        forwards.extend(copy for copy, _, _ in sent)
        return sent

    def arrived(q, sent):
        for _, index, t in sent:
            other = other_rows(t)
            pltpu.make_async_remote_copy(
                src_ref=remote.at[q, other, :],
                dst_ref=remote.at[q, other, :],
                send_sem=send_sem.at[index],
                recv_sem=recv_sem.at[index],
                device_id=me_sibling,
                device_id_type=MESH,
            ).wait_recv()

    release(False)
    for copy in row_halo:
        copy.wait_recv()
    over(both_first, 0, last, 2)

    @pl.when(calm)
    def _():
        for copy in held_last:
            copy.start()

    solids_sent = forward(0)

    @pl.when(jnp.logical_or(higher[PARTNER], patient))
    def _():
        for copy in held_last:
            copy.start()

    arrived(0, solids_sent)

    def section_one_own(r, j):
        section_one(r, j, total[(0, *at(r, j))] + remote[(0, *at(r, j))], True)

    over(section_one_own, 0, 1, row_tiles, unroll=8)
    pack_cols(first, classes + 1, pack, 4, own_tiles)
    col_halo_one = send_cols(pack, 4, None, None)

    for copy in edge_sums + corners:
        copy.wait_recv()
    unpack_cols(field, classes + 3, corner, 0, outer_tiles, walls)
    for side, r in ((-1, -1), (1, row_tiles)):

        def outer(_, j, side=side, r=r):
            coefficients(r, j, side)
            carry_first(r, j, side)
            low = 0 if side < 0 else 1
            strip = pl.ds(pl.multiple_of(j * LANE, LANE), LANE)
            section_one(r, j, edges[0, low, :, strip] + edges[1, low, :, strip], False)

        over(outer, r, 1, 1, unroll=2)

    def carry_second(r, j):
        factors = [coef[(i, *at(r + 1, j))] for i in range(5)]
        for k in range(classes):
            value = tile(field, k, r, j) + transported(first, k, r, j, factors)
            out[(k, *at(r, j))] = 0.5 * value
        moved[at(r, j)] = transported(first, classes, r, j, factors)

    over(carry_second, 0, 1, row_tiles, 1, 1, col_tiles - 2)
    weighted_sent = forward(1)
    for copy in col_halo_one:
        copy.wait_recv()
    unpack_cols(first, classes + 1, pack, 6, own_tiles, ())
    over(carry_second, 0, 1, row_tiles, 0, col_tiles - 1, 2)
    arrived(1, weighted_sent)

    def finish(r, j):
        weighted = total[(1, *at(r, j))] + remote[(1, *at(r, j))]
        solids = moved[at(r, j)] - gain[at(r, j)] * weighted
        g = (0.5 * tile(field, classes + BED, r, j)) * hindered(solids)
        for k in range(classes):
            out[(k, *at(r, j))] = out[(k, *at(r, j))] - (speed[k] * g) * tile(first, k, r, j)

    over(finish, 0, 1, row_tiles, unroll=8)

    for copy in far + edge_sums + row_halo + col_halo + corners + forwards + col_halo_one:
        copy.wait_send()


def per_device(concentration, class_table, settle_speed, along_speed, across_speed, film_depth, cell_mask):
    classes, rows, cols = concentration.shape
    padded = (rows + 2 * SUB, cols + 2 * LANE)
    flat = (rows, cols)
    row_tiles = rows // SUB
    copies = 2 + 4 * (row_tiles // 2) + 14
    anywhere = pl.BlockSpec(memory_space=pl.ANY)
    f32 = jnp.float32

    def keep(array):
        return pltpu.with_memory_space_constraint(array, pltpu.HBM)

    return pl.pallas_call(
        section_kernel,
        out_shape=pltpu.VMEM(concentration.shape, f32),
        in_specs=[anywhere] * 7,
        out_specs=pl.BlockSpec(memory_space=pltpu.VMEM),
        scratch_shapes=[
            pltpu.SMEM(class_table.shape, jnp.int32),
            pltpu.SMEM(settle_speed.shape, f32),
            pltpu.VMEM((classes + 4, *padded), f32),
            pltpu.VMEM((classes + 1, *padded), f32),
            pltpu.VMEM((2, 2, SUB, cols), f32),
            pltpu.VMEM((2, *flat), f32),
            pltpu.VMEM((2, *flat), f32),
            pltpu.VMEM((2, *flat), f32),
            pltpu.VMEM((2, *flat), f32),
            pltpu.VMEM((5, rows + 2 * SUB, cols), f32),
            pltpu.VMEM(flat, f32),
            pltpu.VMEM(flat, f32),
            pltpu.VMEM(flat, f32),
            pltpu.VMEM(flat, jnp.int32),
            pltpu.VMEM((8, rows, LANE), f32),
            pltpu.VMEM((2, 2 * SUB, LANE), f32),
            pltpu.SemaphoreType.DMA((row_tiles + 6,)),
            pltpu.SemaphoreType.DMA((copies,)),
            pltpu.SemaphoreType.DMA((copies,)),
            pltpu.SemaphoreType.REGULAR((11,)),
        ],
        compiler_params=pltpu.CompilerParams(
            collective_id=0, has_side_effects=True, vmem_limit_bytes=32 * 2**20
        ),
        cost_estimate=pl.CostEstimate(
            flops=40 * classes * rows * cols, bytes_accessed=8 * classes * rows * cols, transcendentals=4 * rows * cols
        ),
    )(*map(keep, (concentration, class_table, settle_speed, along_speed, across_speed, film_depth, cell_mask)))


def solution(mesh):
    grid = P("helix", "cross")
    return jax.shard_map(
        per_device,
        mesh=mesh,
        in_specs=(P("cls", "helix", "cross"), P("cls"), P(), grid, grid, grid, grid),
        out_specs=P("cls", "helix", "cross"),
        check_vma=False,
    )
```
